256 devices in a mesh: batch: 64 (over x, z, core), mp: 4 (over y).
Axes of the slice: x: 4, y: 4, z: 8, core: 2. Of those that a mesh axis runs over, the one named last changes fastest.
Arguments:
- query_hidden: bfloat16 [16384, 4096], P('batch', 'mp'), may hold values from -6 to 6
- positive_hidden: bfloat16 [16384, 4096], P('batch', 'mp'), may hold values from -6 to 6
- pool_hidden: bfloat16 [32768, 4096], P('batch', 'mp'), may hold values from -6 to 6
- norm_gain: float32 [4096], P('mp'), may hold values from 0.1 to 1.9
- hard_ids: int32 [16384, 3], P('batch'), may hold values from 0 to 32767, as said below
- location: int32 [32768], replicated, may hold values from 0 to 32767, as said below
- partner_masks: int32 [2], replicated, may hold values from 1 to 63
Outputs:
- query_loss: float32 [16384], P(('batch', 'mp'))
- grad_query: bfloat16 [16384, 4096], P('batch', 'mp')
- grad_positive: bfloat16 [16384, 4096], P('batch', 'mp')
- grad_pool: bfloat16 [32768, 4096], P('batch', 'mp')
The draws below stay inside these ranges and needn't reach their ends.
Inputs may be any that keep to these rules, and one draw needn't show every extreme that they name: `hard_ids`: every entry is a passage id. With owner(p) = location[p] // 512: the 768 ids of the queries of one batch device are all different, at most 24 of them have one owner, and some owner is named exactly 24 times by the queries of every batch device. A permutation: passage id p is stored at row location[p] of the pool.
All inputs are finite; a program needn't handle non-finite values.
Results may differ from the reference program's by a relative error of at most 0.0073.
Values may be sent and summed in bfloat16 or wider, within the bound.
No kernel may reach another device: no remote copies, remote signals or barrier semaphores. Data moves between devices by JAX's collectives and lax.ppermute only.
A program may use at most 64 MiB of HBM per device.

```python
import jax
import jax.numpy as jnp
from jax import lax

MODEL_WIDTH = 4096
Q_DEV = 256
HARD = 3
MATCHINGS = 2
POOL_DEV = 512
CAP = 24
QUERIES = 16384
POOL = 32768
N_BATCH = 64


def hard_layout(key):
    devices = N_BATCH
    hard_count = HARD * Q_DEV
    key_hot, key_owner, key_base, key_order, key_perm = jax.random.split(key, 5)
    hottest = jax.random.randint(key_hot, (), 0, devices)
    orders = jax.vmap(lambda single: jax.random.permutation(single, devices))(jax.random.split(key_owner, devices))
    leading = orders[:, :1]
    orders = jnp.where(orders == hottest, leading, orders)
    orders = orders.at[:, 0].set(hottest)
    slots = jnp.arange(hard_count, dtype=jnp.int32)
    others = max(devices - 1, 1)
    beyond = jnp.maximum(slots - CAP, 0)
    ranking = jnp.where(slots < CAP, 0, 1 + beyond % others)
    within = jnp.where(slots < CAP, slots, beyond // others)
    owners = jnp.take_along_axis(orders, jnp.broadcast_to(ranking, (devices, hard_count)), axis=1)
    bases = jax.random.randint(key_base, (devices, devices), 0, POOL_DEV)
    starts = jnp.take_along_axis(bases, owners, axis=1)
    storage = owners * POOL_DEV + (starts + within[None, :]) % POOL_DEV
    shuffles = jax.vmap(lambda single: jax.random.permutation(single, hard_count))(jax.random.split(key_order, devices))
    storage = jnp.take_along_axis(storage, shuffles, axis=1)
    placement = jax.random.permutation(key_perm, POOL)
    return (storage, placement)


def draw_location(key, part):
    storage, placement = hard_layout(key)
    return placement.astype(jnp.int32)


def draw_hard_ids(key, part):
    storage, placement = hard_layout(key)
    passage_of_row = jnp.argsort(placement)
    return passage_of_row[storage].reshape(QUERIES, HARD).astype(jnp.int32)


def block_levels(own_key, extent, cuts, low, high):
    loudness = 1.0
    for axis_at, parts in cuts:
        draws = jax.random.uniform(jax.random.fold_in(jax.random.fold_in(own_key, 6), axis_at), (parts,), jnp.float32, low / len(cuts), high / len(cuts))
        loudness = loudness * jnp.repeat(jnp.exp(draws), extent[axis_at] // parts).reshape((-1,) + (1,) * (len(extent) - 1 - axis_at))
    return loudness


def gaussian(stream_key, dims, deviation, reach, cuts=(), held_as=jnp.bfloat16):
    entries = jax.random.normal(stream_key, dims, jnp.float32) * deviation
    if len(cuts) > 0:
        entries = block_levels(stream_key, dims, cuts, -0.22, 0.18) * entries
    return jnp.clip(entries, min=-reach, max=reach).astype(held_as)


def setup_inputs(seed: int = 0) -> dict:
    seeds = jax.random.split(jax.random.key(seed), 8)
    query_hidden = gaussian(seeds[0], (QUERIES, MODEL_WIDTH), 1.0, 6.0, ((0, 64), (1, 4)))
    positive_hidden = gaussian(seeds[1], (QUERIES, MODEL_WIDTH), 1.0, 6.0, ((0, 64), (1, 4)))
    pool_hidden = gaussian(seeds[2], (POOL, MODEL_WIDTH), 1.0, 6.0, ((0, 64), (1, 4)))
    norm_gain = jnp.clip(1.0 + 0.18 * jax.random.normal(seeds[3], (MODEL_WIDTH,), jnp.float32), 0.1, 1.9)
    hard_ids = draw_hard_ids(jax.random.fold_in(seeds[7], 71), 0)
    location = draw_location(jax.random.fold_in(seeds[7], 71), 0)
    partner_masks = jax.random.randint(seeds[6], (MATCHINGS,), 1, N_BATCH).astype(jnp.int32)
    return {"query_hidden": query_hidden, "positive_hidden": positive_hidden, "pool_hidden": pool_hidden, "norm_gain": norm_gain, "hard_ids": hard_ids, "location": location, "partner_masks": partner_masks}


SOFTMAX_TEMPER = 0.02
EPSILON = 1e-06

def embedding(hidden, norm_gain):
    scaled = norm_gain[None, :] * hidden.astype(jnp.float32)
    inverse = lax.rsqrt(lax.optimization_barrier(jnp.sum(scaled * scaled, axis=1)) + EPSILON)
    return (scaled, inverse, (scaled * inverse[:, None]).astype(jnp.bfloat16))

def gradient(scaled, inverse, delta, norm_gain):
    product = lax.optimization_barrier(jnp.sum(scaled * delta, axis=1))
    inner = delta - scaled * (inverse * inverse * product)[:, None]
    return (norm_gain[None, :] * inverse[:, None] * inner).astype(jnp.bfloat16)

def through_bf16(value):
    rounded = lax.optimization_barrier(value.astype(jnp.bfloat16))
    return rounded.astype(jnp.float32)

def reference(query_hidden, positive_hidden, pool_hidden, norm_gain, hard_ids, location, partner_masks):
    scaled_q, inverse_q, emb_q = embedding(query_hidden, norm_gain)
    scaled_p, inverse_p, emb_p = embedding(positive_hidden, norm_gain)
    scaled_pool, inverse_pool, emb_pool = embedding(pool_hidden, norm_gain)
    query_blocks = emb_q.reshape(N_BATCH, Q_DEV, MODEL_WIDTH)
    blocks_p = emb_p.reshape(N_BATCH, Q_DEV, MODEL_WIDTH)
    storage = location[hard_ids.reshape(N_BATCH, HARD * Q_DEV)]
    devices = jnp.arange(N_BATCH, dtype=jnp.int32)
    partner_one = jnp.bitwise_xor(devices, partner_masks[0])
    partner_two = jnp.bitwise_xor(devices, partner_masks[1])
    scale_factor = MODEL_WIDTH / 64.0 / SOFTMAX_TEMPER
    columns = (HARD + 3) * Q_DEV
    target = (jnp.arange(Q_DEV)[:, None] == jnp.arange(columns)[None, :]).astype(jnp.float32)

    def forward(accelerator_index):
        candidate_rows = jnp.concatenate([blocks_p[accelerator_index], blocks_p[partner_one[accelerator_index]], blocks_p[partner_two[accelerator_index]], emb_pool[storage[accelerator_index]]], axis=0)
        similarity_logits = lax.dot_general(query_blocks[accelerator_index], candidate_rows, (((1,), (1,)), ((), ())), preferred_element_type=jnp.float32) / SOFTMAX_TEMPER
        totals = jnp.log(lax.optimization_barrier(jnp.sum(jnp.exp(similarity_logits), axis=1)))
        losses = totals - jnp.diagonal(similarity_logits[:, :Q_DEV])
        weights = ((jnp.exp(similarity_logits - totals[:, None]) - target) * scale_factor).astype(jnp.bfloat16)
        delta_q = jnp.dot(weights, candidate_rows, preferred_element_type=jnp.float32)
        return (losses, delta_q, weights)
    losses, deltas_q, weights = lax.map(forward, devices)

    def block_term(accelerator_index, first):
        part = weights[accelerator_index][:, first:first + Q_DEV]
        return lax.dot_general(part, query_blocks[accelerator_index], (((0,), (0,)), ((), ())), preferred_element_type=jnp.float32)

    def positive_term(accelerator_index):
        own = block_term(accelerator_index, 0)
        from_one = through_bf16(block_term(partner_one[accelerator_index], Q_DEV))
        from_two = through_bf16(block_term(partner_two[accelerator_index], 2 * Q_DEV))
        return own + from_one + from_two
    deltas_p = lax.map(positive_term, devices)

    def pool_step(total, accelerator_index):
        part = weights[accelerator_index][:, 3 * Q_DEV:]
        term = lax.dot_general(part, query_blocks[accelerator_index], (((0,), (0,)), ((), ())), preferred_element_type=jnp.float32)
        return (total.at[storage[accelerator_index]].add(through_bf16(term)), None)
    delta_pool, unused = lax.scan(pool_step, jnp.zeros((POOL, MODEL_WIDTH), jnp.float32), devices)
    grad_query = gradient(scaled_q, inverse_q, deltas_q.reshape(QUERIES, MODEL_WIDTH), norm_gain)
    grad_positive = gradient(scaled_p, inverse_p, deltas_p.reshape(QUERIES, MODEL_WIDTH), norm_gain)
    grad_pool = gradient(scaled_pool, inverse_pool, delta_pool, norm_gain)
    return (losses.reshape(QUERIES), grad_query, grad_positive, grad_pool)
```

```python
import jax
import jax.numpy as jnp
from jax import lax
from jax.sharding import PartitionSpec as P

MODEL_WIDTH = 4096
SOFTMAX_TEMPER = 0.02
EPSILON = 1e-06
SCALE = MODEL_WIDTH / 64.0 / SOFTMAX_TEMPER
BF = jnp.bfloat16
F32 = jnp.float32


def exchanged(x):
    return lax.all_to_all(x, "batch", split_axis=0, concat_axis=0, tiled=True)


def scaled_rows(hidden, norm_gain):
    return norm_gain[None, :] * hidden.astype(F32)


def row_squares(hidden, norm_gain):
    scaled = scaled_rows(hidden, norm_gain)
    return jnp.sum(scaled * scaled, axis=1)


def embedding(hidden, norm_gain, inverse):
    return (scaled_rows(hidden, norm_gain) * inverse[:, None]).astype(BF)


def gradient(hidden, inverse, delta, product, norm_gain):
    inner = delta - scaled_rows(hidden, norm_gain) * (inverse * inverse * product)[:, None]
    return (norm_gain[None, :] * inverse[:, None] * inner).astype(BF)


def dot(a, b, dims=((1,), (0,))):
    return lax.dot_general(a, b, (dims, ((), ())), preferred_element_type=F32)


def one_hot(column, width):
    return (column[:, None] == jnp.arange(width, dtype=jnp.int32)[None, :]).astype(BF)


def looked_up(table, ids):
    rows = table.shape[0] // 128
    bytes_of = table.reshape(rows, 128)
    parts = jnp.concatenate([bytes_of >> 8, bytes_of & 255], axis=1).astype(BF)
    found = dot(one_hot(ids >> 7, rows), parts)
    value = found[:, :128] * 256.0 + found[:, 128:]
    lane = (ids & 127)[:, None] == jnp.arange(128, dtype=jnp.int32)[None, :]
    return jnp.sum(jnp.where(lane, value, 0.0), axis=1).astype(jnp.int32)


def summed(x):
    parts = lax.axis_size("mp")
    total = x
    for step in range(1, parts):
        total = total + lax.ppermute(x, "mp", [(i, (i + step) % parts) for i in range(parts)])
    return total


def per_device(
    query_hidden, positive_hidden, pool_hidden, norm_gain, hard_ids, location, partner_masks
):
    devices = lax.axis_size("batch")
    parts = lax.axis_size("mp")
    me_mp = lax.axis_index("mp")
    rows_dev, feature_dev = query_hidden.shape
    pool_dev = pool_hidden.shape[0]
    hard_count = hard_ids.shape[0] * hard_ids.shape[1]
    capacity = max(hard_count // 32, 2 * ((hard_count + devices - 1) // devices))
    chunk = rows_dev // devices
    block = capacity + 2 * chunk
    slots = devices * block
    share = rows_dev // parts
    int_range = lambda n: jnp.arange(n, dtype=jnp.int32)

    inverse_p = lax.rsqrt(summed(row_squares(positive_hidden, norm_gain)) + EPSILON)
    emb_p = embedding(positive_hidden, norm_gain, inverse_p)

    ids = hard_ids.T.reshape(-1)
    storage = looked_up(location, ids)
    owners = storage // pool_dev
    local_row = storage % pool_dev
    order = int_range(hard_count)
    earlier = (owners[:, None] == owners[None, :]) & (order[None, :] < order[:, None])
    slot_index = jnp.sum(earlier.astype(jnp.int32), axis=1)
    position = owners * block + slot_index
    lane = slot_index // chunk
    lanes = int_range(128)[None, :]
    wanted = local_row + 1
    digits = jnp.where(
        lanes == lane[:, None],
        (wanted >> 4)[:, None],
        jnp.where(lanes == lane[:, None] + 64, (wanted & 15)[:, None], 0),
    ).astype(BF)
    line = one_hot(owners * chunk + slot_index % chunk, devices * chunk)
    requests = dot(line, digits, ((0,), (0,))).astype(BF)

    first = exchanged(
        jnp.concatenate(
            [
                emb_p.reshape(devices, chunk, feature_dev),
                requests.reshape(devices, chunk, 128),
            ],
            axis=2,
        )
    )
    spread = first[:, :, :feature_dev].reshape(rows_dev, feature_dev)
    steps = capacity // chunk
    asked = first[:, :, feature_dev:].astype(jnp.int32)
    asked = asked[:, :, :steps] * 16 + asked[:, :, 64 : 64 + steps] - 1
    asked = jnp.swapaxes(asked, 1, 2).reshape(devices, capacity)

    inverse_q, inverse_pool = (
        lax.rsqrt(x + EPSILON)
        for x in jnp.split(
            summed(
                jnp.concatenate(
                    [row_squares(query_hidden, norm_gain), row_squares(pool_hidden, norm_gain)]
                )
            ),
            [rows_dev],
        )
    )
    emb_q = embedding(query_hidden, norm_gain, inverse_q)
    emb_pool = embedding(pool_hidden, norm_gain, inverse_pool)
    turned_q = lax.dynamic_slice_in_dim(
        jnp.concatenate([emb_q, emb_q], axis=0), me_mp * share, rows_dev
    )

    source = (int_range(devices)[:, None] ^ partner_masks[None, :])[:, :, None] * chunk
    source = (source + int_range(chunk)[None, None, :]).reshape(devices, 2 * chunk)
    taken = jnp.concatenate([asked, source + pool_dev], axis=1).reshape(-1)
    serve = one_hot(taken, pool_dev + rows_dev)
    served = dot(serve, jnp.concatenate([emb_pool, spread], axis=0)).astype(BF)
    second = exchanged(served.reshape(devices, block, feature_dev))
    arrived = second.reshape(slots, feature_dev)

    hard_emb = dot(one_hot(position, slots), arrived).astype(BF)
    far = jnp.concatenate(
        [second[:, capacity:].reshape(2 * rows_dev, feature_dev), hard_emb], axis=0
    )
    far_slot = jnp.concatenate(
        [
            (int_range(devices)[:, None] * block + capacity + int_range(2 * chunk)[None, :]).reshape(
                -1
            ),
            position,
        ]
    )

    def shared_scores(candidates):
        total = dot(turned_q[:share], candidates, ((1,), (1,)))
        for step in range(1, parts):
            piece = dot(turned_q[step * share : (step + 1) * share], candidates, ((1,), (1,)))
            total = total + lax.ppermute(
                piece, "mp", [(i, (i + step) % parts) for i in range(parts)]
            )
        return total / SOFTMAX_TEMPER

    scores_own = shared_scores(emb_p)
    scores_far = shared_scores(far)
    exp_own = jnp.exp(scores_own)
    exp_far = jnp.exp(scores_far)
    sums = jnp.sum(exp_own, axis=1) + jnp.sum(exp_far, axis=1)
    own = int_range(share)[:, None] + me_mp * share == int_range(rows_dev)[None, :]
    losses = jnp.log(sums) - jnp.sum(jnp.where(own, scores_own, 0.0), axis=1)
    ratio = 1.0 / sums
    weights_own = ((exp_own * ratio[:, None] - own.astype(F32)) * SCALE).astype(BF)
    weights_far = (exp_far * ratio[:, None] * SCALE).astype(BF)

    def gathered(piece):
        pieces = [piece]
        for step in range(1, parts):
            pieces.append(
                lax.ppermute(piece, "mp", [((i + step) % parts, i) for i in range(parts)])
            )
        return jnp.concatenate(pieces, axis=0)

    weights_far = gathered(weights_far)
    weights_own = gathered(weights_own)

    weights_slots = dot(weights_far, one_hot(far_slot, slots)).astype(BF)
    outgoing = dot(weights_slots, turned_q, ((0,), (0,))).astype(BF)
    third = exchanged(outgoing.reshape(devices, block, feature_dev)).reshape(slots, feature_dev)
    merged = dot(serve[:, pool_dev:], third, ((0,), (0,))).astype(BF)
    home = exchanged(merged.reshape(devices, chunk, feature_dev)).reshape(rows_dev, feature_dev)

    def natural(x):
        return lax.dynamic_slice_in_dim(
            jnp.concatenate([x, x], axis=0), (parts - me_mp) * share, rows_dev
        )

    delta_q = natural(dot(weights_own, emb_p) + dot(weights_slots, arrived))
    delta_p = dot(weights_own, turned_q, ((0,), (0,))) + home.astype(F32)
    delta_pool = dot(serve[:, :pool_dev], third, ((0,), (0,)))

    def finished(hidden, inverse, delta):
        product = summed(jnp.sum(scaled_rows(hidden, norm_gain) * delta, axis=1))
        return gradient(hidden, inverse, delta, product, norm_gain)

    return (
        losses,
        finished(query_hidden, inverse_q, delta_q),
        finished(positive_hidden, inverse_p, delta_p),
        finished(pool_hidden, inverse_pool, delta_pool),
    )


def solution(mesh):
    placed = (
        P("batch", "mp"),
        P("batch", "mp"),
        P("batch", "mp"),
        P("mp"),
        P("batch", None),
        P(),
        P(),
    )
    return jax.shard_map(
        per_device,
        mesh=mesh,
        in_specs=placed,
        out_specs=(P(("batch", "mp")), P("batch", "mp"), P("batch", "mp"), P("batch", "mp")),
        check_vma=False,
    )
```

```python
import jax
import jax.numpy as jnp
from jax import lax
from jax.sharding import PartitionSpec as P

MODEL_WIDTH = 4096
SOFTMAX_TEMPER = 0.02
EPSILON = 1e-06
FIXED = 32000.0
SCALE = MODEL_WIDTH / 64.0 / SOFTMAX_TEMPER
BF = jnp.bfloat16
F32 = jnp.float32


def exchanged(x):
    return lax.all_to_all(x, "batch", split_axis=0, concat_axis=0, tiled=True)


def scaled_rows(hidden, norm_gain):
    return norm_gain[None, :] * hidden.astype(F32)


def row_squares(hidden, norm_gain):
    scaled = scaled_rows(hidden, norm_gain)
    return jnp.sum(scaled * scaled, axis=1)


def embedding(hidden, norm_gain, inverse):
    return (scaled_rows(hidden, norm_gain) * inverse[:, None]).astype(BF)


def gradient(hidden, inverse, delta, product, norm_gain):
    inner = delta - scaled_rows(hidden, norm_gain) * (inverse * inverse * product)[:, None]
    return (norm_gain[None, :] * inverse[:, None] * inner).astype(BF)


def dot(a, b, dims=((1,), (0,))):
    return lax.dot_general(a, b, (dims, ((), ())), preferred_element_type=F32)


def one_hot(column, width):
    return (column[:, None] == jnp.arange(width, dtype=jnp.int32)[None, :]).astype(BF)


def looked_up(table, ids):
    rows = table.shape[0] // 128
    bytes_of = table.reshape(rows, 128)
    parts = jnp.concatenate([bytes_of >> 8, bytes_of & 255], axis=1).astype(BF)
    found = dot(one_hot(ids >> 7, rows), parts)
    value = found[:, :128] * 256.0 + found[:, 128:]
    lane = (ids & 127)[:, None] == jnp.arange(128, dtype=jnp.int32)[None, :]
    return jnp.sum(jnp.where(lane, value, 0.0), axis=1).astype(jnp.int32)


def after(x, value):
    return jnp.where(jnp.isnan(value.reshape(-1)[0].astype(F32)), jnp.zeros_like(x), x)


def summed(x):
    parts = lax.axis_size("mp")
    total = x
    for step in range(1, parts):
        total = total + lax.ppermute(x, "mp", [(i, (i + step) % parts) for i in range(parts)])
    return total


def per_device(
    query_hidden, positive_hidden, pool_hidden, norm_gain, hard_ids, location, partner_masks
):
    devices = lax.axis_size("batch")
    parts = lax.axis_size("mp")
    me_mp = lax.axis_index("mp")
    rows_dev, feature_dev = query_hidden.shape
    pool_dev = pool_hidden.shape[0]
    hard_count = hard_ids.shape[0] * hard_ids.shape[1]
    capacity = max(hard_count // 32, 2 * ((hard_count + devices - 1) // devices))
    chunk = rows_dev // devices
    block = capacity + 2 * chunk
    slots = devices * block
    share = rows_dev // parts
    int_range = lambda n: jnp.arange(n, dtype=jnp.int32)

    partial_squares = jnp.concatenate(
        [row_squares(x, norm_gain) for x in (positive_hidden, query_hidden, pool_hidden)]
    )
    inverse = lax.rsqrt(summed(partial_squares) + EPSILON)
    inverse_p, inverse_q, inverse_pool = jnp.split(inverse, [rows_dev, 2 * rows_dev])
    emb_p = embedding(positive_hidden, norm_gain, inverse_p)

    ids = after(hard_ids, partial_squares).T.reshape(-1)
    storage = looked_up(location, ids)
    owners = storage // pool_dev
    local_row = storage % pool_dev
    order = int_range(hard_count)
    earlier = (owners[:, None] == owners[None, :]) & (order[None, :] < order[:, None])
    slot_index = jnp.sum(earlier.astype(jnp.int32), axis=1)
    position = owners * block + slot_index
    lane = slot_index // chunk
    lanes = int_range(128)[None, :]
    wanted = local_row + 1
    digits = jnp.where(
        lanes == lane[:, None],
        (wanted >> 4)[:, None],
        jnp.where(lanes == lane[:, None] + 64, (wanted & 15)[:, None], 0),
    ).astype(BF)
    line = one_hot(owners * chunk + slot_index % chunk, devices * chunk)
    requests = dot(line, digits, ((0,), (0,))).astype(BF)

    first = exchanged(
        jnp.concatenate(
            [
                emb_p.reshape(devices, chunk, feature_dev),
                requests.reshape(devices, chunk, 128),
            ],
            axis=2,
        )
    ).reshape(rows_dev, feature_dev + 128)
    spread = first[:, :feature_dev]
    steps = capacity // chunk
    asked = first[:, feature_dev:].reshape(devices, chunk, 128).astype(jnp.int32)
    asked = asked[:, :, :steps] * 16 + asked[:, :, 64 : 64 + steps] - 1
    asked = jnp.swapaxes(asked, 1, 2).reshape(devices, capacity)

    emb_q = embedding(query_hidden, norm_gain, inverse_q)
    emb_pool = embedding(pool_hidden, norm_gain, inverse_pool)
    turned_q = lax.dynamic_slice_in_dim(
        jnp.concatenate([emb_q, emb_q], axis=0), me_mp * share, rows_dev
    )

    source = (int_range(devices)[:, None] ^ partner_masks[None, :])[:, :, None] * chunk
    source = (source + int_range(chunk)[None, None, :]).reshape(devices, 2 * chunk)
    taken = jnp.concatenate([asked, source + pool_dev], axis=1).reshape(-1)
    serve = one_hot(taken, pool_dev + rows_dev)
    served = dot(serve, jnp.concatenate([emb_pool, spread], axis=0)).astype(BF)
    arrived = exchanged(served)
    partner_emb = arrived.reshape(devices, block, feature_dev)[:, capacity:].reshape(
        2 * rows_dev, feature_dev
    )
    far_slot = jnp.concatenate(
        [
            (int_range(devices)[:, None] * block + capacity + int_range(2 * chunk)[None, :]).reshape(
                -1
            ),
            position,
        ]
    )

    def sent_scores(candidates):
        partial = dot(turned_q[share:], candidates, ((1,), (1,)))
        coded = jnp.round(partial * FIXED).astype(jnp.int16)
        total = 0.0
        for step in range(1, parts):
            total = total + lax.ppermute(
                coded[(step - 1) * share : step * share],
                "mp",
                [(i, (i + step) % parts) for i in range(parts)],
            ).astype(F32)
        return coded, total

    def shared_scores(candidates, total):
        kept = dot(turned_q[:share], candidates, ((1,), (1,)))
        return (kept + total * (1.0 / FIXED)) * (1.0 / SOFTMAX_TEMPER)

    own_parts = dot(turned_q, emb_p, ((1,), (1,)))
    scores_own = own_parts[:share]
    for step in range(1, parts):
        scores_own = scores_own + lax.ppermute(
            own_parts[step * share : (step + 1) * share],
            "mp",
            [(i, (i + step) % parts) for i in range(parts)],
        )
    scores_own = scores_own / SOFTMAX_TEMPER
    coded, total_partner = sent_scores(partner_emb)
    hard_emb = dot(one_hot(after(position, coded), slots), arrived).astype(BF)
    coded, total_hard = sent_scores(hard_emb)
    scores_far = jnp.concatenate(
        [
            shared_scores(partner_emb, total_partner),
            shared_scores(hard_emb, total_hard),
        ],
        axis=1,
    )
    exp_own = jnp.exp(scores_own)
    exp_far = jnp.exp(scores_far)
    sums = jnp.sum(exp_own, axis=1) + jnp.sum(exp_far, axis=1)
    own = int_range(share)[:, None] + me_mp * share == int_range(rows_dev)[None, :]
    losses = jnp.log(sums) - jnp.sum(jnp.where(own, scores_own, 0.0), axis=1)
    ratio = 1.0 / sums
    weights_own = ((exp_own * ratio[:, None] - own.astype(F32)) * SCALE).astype(BF)
    weights_far = (exp_far * ratio[:, None] * SCALE).astype(BF)

    def gathered(piece):
        pieces = [piece]
        for step in range(1, parts):
            pieces.append(
                lax.ppermute(piece, "mp", [((i + step) % parts, i) for i in range(parts)])
            )
        return jnp.concatenate(pieces, axis=0)

    weights_far = gathered(weights_far)
    weights_own = gathered(weights_own)

    weights_slots = dot(weights_far, one_hot(far_slot, slots)).astype(BF)
    outgoing = dot(weights_slots, turned_q, ((0,), (0,))).astype(BF)
    third = exchanged(outgoing)

    def natural(x):
        return lax.dynamic_slice_in_dim(
            jnp.concatenate([x, x], axis=0), (parts - me_mp) * share, rows_dev
        )

    def row_products(hidden, delta):
        return summed(jnp.sum(scaled_rows(hidden, norm_gain) * delta, axis=1))

    delta_q = natural(dot(weights_own, emb_p) + dot(weights_slots, arrived))
    product_q = row_products(query_hidden, delta_q)
    grad_q = gradient(query_hidden, inverse_q, delta_q, product_q, norm_gain)
    delta_own = dot(weights_own, turned_q, ((0,), (0,)))

    back = one_hot(after(after(taken, grad_q), delta_own), pool_dev + rows_dev)
    merged = dot(back[:, pool_dev:], third, ((0,), (0,))).astype(BF)
    home = exchanged(merged)
    delta_pool = dot(back[:, :pool_dev], third, ((0,), (0,)))
    product_pool = row_products(pool_hidden, delta_pool)
    grad_pool = gradient(pool_hidden, inverse_pool, delta_pool, product_pool, norm_gain)
    delta_p = delta_own + home.astype(F32)
    product_p = row_products(positive_hidden, delta_p)
    grad_p = gradient(positive_hidden, inverse_p, delta_p, product_p, norm_gain)
    return (losses, grad_q, grad_p, grad_pool)


def solution(mesh):
    placed = (
        P("batch", "mp"),
        P("batch", "mp"),
        P("batch", "mp"),
        P("mp"),
        P("batch", None),
        P(),
        P(),
    )
    return jax.shard_map(
        per_device,
        mesh=mesh,
        in_specs=placed,
        out_specs=(P(("batch", "mp")), P("batch", "mp"), P("batch", "mp"), P("batch", "mp")),
        check_vma=False,
    )
```

```python
import jax
import jax.numpy as jnp
from jax import lax
from jax.experimental import pallas as pl
from jax.experimental.pallas import tpu as pltpu
from jax.sharding import PartitionSpec as P

MODEL_WIDTH = 4096
SOFTMAX_TEMPER = 0.02
EPSILON = 1e-06
FIXED = 32000.0
SCALE = MODEL_WIDTH / 64.0 / SOFTMAX_TEMPER
BF = jnp.bfloat16
F32 = jnp.float32


def exchanged(x):
    return lax.all_to_all(x, "batch", split_axis=0, concat_axis=0, tiled=True)


def scaled_rows(hidden, norm_gain):
    return norm_gain[None, :] * hidden.astype(F32)


def row_squares(hidden, norm_gain):
    scaled = scaled_rows(hidden, norm_gain)
    return jnp.sum(scaled * scaled, axis=1)


def embedding(hidden, norm_gain, inverse):
    return (scaled_rows(hidden, norm_gain) * inverse[:, None]).astype(BF)


def gradient(hidden, inverse, delta, product, norm_gain):
    inner = delta - scaled_rows(hidden, norm_gain) * (inverse * inverse * product)[:, None]
    return (norm_gain[None, :] * inverse[:, None] * inner).astype(BF)


def dot(a, b, dims=((1,), (0,))):
    return lax.dot_general(a, b, (dims, ((), ())), preferred_element_type=F32)


def one_hot(column, width):
    return (column[:, None] == jnp.arange(width, dtype=jnp.int32)[None, :]).astype(BF)


def looked_up(table, ids):
    rows = table.shape[0] // 128
    bytes_of = table.reshape(rows, 128)
    parts = jnp.concatenate([bytes_of >> 8, bytes_of & 255], axis=1).astype(BF)
    found = dot(one_hot(ids >> 7, rows), parts)
    value = found[:, :128] * 256.0 + found[:, 128:]
    lane = (ids & 127)[:, None] == jnp.arange(128, dtype=jnp.int32)[None, :]
    return jnp.sum(jnp.where(lane, value, 0.0), axis=1).astype(jnp.int32)


def after(x, value):
    return jnp.where(jnp.isnan(value.reshape(-1)[0].astype(F32)), jnp.zeros_like(x), x)


def summed(x):
    parts = lax.axis_size("mp")
    total = x
    for step in range(1, parts):
        total = total + lax.ppermute(x, "mp", [(i, (i + step) % parts) for i in range(parts)])
    return total


VMEM_BYTES = 40 * 1024 * 1024
GROUP = 8


def called(body, out_shape, flops, **more):
    return pl.pallas_call(
        body,
        out_shape=out_shape,
        compiler_params=pltpu.CompilerParams(vmem_limit_bytes=VMEM_BYTES),
        cost_estimate=pl.CostEstimate(flops=flops, bytes_accessed=8 << 20, transcendentals=0),
        **more,
    )


def lanes_of(shape):
    return lax.broadcasted_iota(jnp.int32, shape, 1)


def sublanes_of(shape):
    return lax.broadcasted_iota(jnp.int32, shape, 0)


def hot(matches):
    return matches.astype(F32).astype(BF)


def whole(shape):
    return pl.BlockSpec(shape, lambda i: (0,) * len(shape))


def split_value(value, lane, at):
    high = value.astype(BF).astype(F32)
    middle = (value - high).astype(BF).astype(F32)
    low = value - high - middle
    return jnp.where(
        lane == at, high, jnp.where(lane == at + 1, middle, jnp.where(lane == at + 2, low, 0.0))
    )


def served_rows(first, emb_pool, masks, steps, chunk):
    rows, width = first.shape
    pool, features = emb_pool.shape
    lines = rows // chunk * GROUP
    halves = GROUP // chunk

    def body(masks_ref, first_ref, pool_ref, out_ref, digits_ref):
        step = pl.program_id(0)
        line = sublanes_of((lines, 1))
        receiver = line // GROUP
        part = (line % GROUP) // chunk
        piece = line % chunk

        @pl.when(step == 0)
        def _():
            spreading = hot(lanes_of((lines, rows)) == receiver * chunk + piece)
            digits_ref[...] = dot(spreading, first_ref[:, features:])

        @pl.when(step < steps)
        def _():
            digits = digits_ref[...]
            lane = lanes_of(digits.shape)
            place = step * halves + part
            value = jnp.where(lane == place, digits * 16.0, 0.0)
            value = jnp.where(lane == place + 64, digits, value)
            asked = jnp.sum(value, axis=1, keepdims=True).astype(jnp.int32) - 1
            out_ref[...] = dot(hot(lanes_of((lines, pool)) == asked), pool_ref[...]).astype(BF)

        @pl.when(step == steps)
        def _():
            mask = jnp.where(part == 0, masks_ref[0], masks_ref[1])
            source = (receiver ^ mask) * chunk + piece
            chosen = hot(lanes_of((lines, rows)) == source)
            out_ref[...] = dot(chosen, first_ref[:, :features]).astype(BF)

    return called(
        body,
        pltpu.HBM((lines, (steps + 1) * features), BF),
        2 * lines * steps * pool * features,
        grid=(steps + 1,),
        in_specs=[
            pl.BlockSpec(memory_space=pltpu.SMEM),
            whole((rows, width)),
            whole((pool, features)),
        ],
        out_specs=pl.BlockSpec((lines, features), lambda i: (0, i)),
        scratch_shapes=[pltpu.VMEM((lines, 128), F32)],
    )(masks, first, emb_pool)


def partial_scores(turned_q, arrived, code, steps, parts):
    rows, features = turned_q.shape
    lines = arrived.shape[0]
    hard = code.shape[0]
    share = rows // parts

    def body(q_ref, arrived_ref, code_ref, emb_ref, kept_ref, *rest):
        *coded_refs, total_ref = rest
        step = pl.program_id(0)

        def score(candidates, at):
            count = candidates.shape[0]
            partial = dot(q_ref[...], candidates, ((1,), (1,)))
            kept_ref[:, at : at + count] = partial[:share]
            for i, ref in enumerate(coded_refs):
                coded = jnp.round(partial[(i + 1) * share : (i + 2) * share] * FIXED)
                ref[:, at : at + count] = coded.astype(jnp.int32).astype(jnp.int16)

        @pl.when(step == 0)
        def _():
            score(arrived_ref[...], 0)
            total_ref[...] = jnp.zeros_like(total_ref)

        @pl.when(step > 0)
        def _():
            chosen = hot(lanes_of((hard, lines)) + (step - 1) * lines == code_ref[...])
            total_ref[...] += dot(chosen, arrived_ref[...])

        @pl.when(step == steps)
        def _():
            emb_ref[...] = total_ref[...].astype(BF)
            score(emb_ref[...], lines)

    columns = lines + hard
    return called(
        body,
        [jax.ShapeDtypeStruct((hard, features), BF), jax.ShapeDtypeStruct((share, columns), F32)]
        + [jax.ShapeDtypeStruct((share, columns), jnp.int16)] * (parts - 1),
        2 * hard * steps * lines * features,
        grid=(steps + 1,),
        in_specs=[
            whole((rows, features)),
            pl.BlockSpec((lines, features), lambda i: (0, (i + steps) % (steps + 1))),
            whole((hard, 1)),
        ],
        out_specs=[whole((hard, features))] + [whole((share, columns))] * parts,
        scratch_shapes=[pltpu.VMEM((hard, features), F32)],
    )(turned_q, arrived, code[:, None])


def outgoing_rows(pieces, code, values, turned_q, lines, steps):
    share, columns = pieces[0].shape
    rows, features = turned_q.shape
    hard = code.shape[0]
    tile = lines // 2

    def body(*refs):
        code_ref, near_ref, far_ref, q_ref, out_ref, all_ref = refs[len(pieces) :]
        step = pl.program_id(0)

        @pl.when(step == 0)
        def _():
            for i, ref in enumerate(refs[: len(pieces)]):
                all_ref[i * share : (i + 1) * share, :] = ref[...]

        lane = lanes_of((tile, 128))
        line = sublanes_of((tile, hard)) + step * tile
        extra = jnp.zeros((tile, 128), F32)
        for t in range(steps):
            matches = line + t * lines == code_ref[...]
            value = jnp.sum(jnp.where(matches, far_ref[...], 0.0), axis=1, keepdims=True)
            extra = extra + split_value(value, lane, 3 * t)
            weights = dot(hot(matches), all_ref[:, lines:], ((1,), (1,))).astype(BF)
            out_ref[:, t * features : (t + 1) * features] = dot(weights, q_ref[...]).astype(BF)
        near = sublanes_of((tile, lines)) + step * tile == lanes_of((tile, lines))
        value = jnp.sum(jnp.where(near, near_ref[...], 0.0), axis=1, keepdims=True)
        extra = extra + split_value(value, lane, 3 * steps)
        weights = all_ref[:, pl.ds(pl.multiple_of(step * tile, tile), tile)]
        delta = dot(weights, q_ref[...], ((0,), (0,)))
        out_ref[:, steps * features : (steps + 1) * features] = delta.astype(BF)
        out_ref[:, (steps + 1) * features :] = extra.astype(BF)

    width = (steps + 1) * features + 128
    return called(
        body,
        pltpu.HBM((lines, width), BF),
        2 * lines * (steps + 1) * rows * (hard + features),
        grid=(2,),
        in_specs=[whole((share, columns))] * len(pieces)
        + [whole((1, hard)), whole((1, lines)), whole((1, hard)), whole((rows, features))],
        out_specs=pl.BlockSpec((tile, width), lambda i: (i, 0)),
        scratch_shapes=[pltpu.VMEM((rows, columns), BF)],
    )(
        *pieces,
        code[None, :],
        values[None, :lines],
        values[None, lines:],
        turned_q,
    )


def merged_rows(third, masks, rows, features, steps, chunk):
    lines, width = third.shape

    def body(masks_ref, near_ref, extra_ref, out_ref):
        line = lanes_of((1, lines))
        mask = jnp.where((line % GROUP) // chunk == 0, masks_ref[0], masks_ref[1])
        target = ((line // GROUP) ^ mask) * chunk + line % chunk
        back = hot(sublanes_of((rows, lines)) == target)
        out_ref[:, :features] = dot(back, near_ref[...]).astype(BF)
        lane = lanes_of((rows, 128))
        terms = dot(back, extra_ref[...])
        mine = (lane >= 3 * steps) & (lane < 3 * steps + 3)
        value = jnp.sum(jnp.where(mine, terms, 0.0), axis=1, keepdims=True)
        out_ref[:, features:] = split_value(value, lane, 0).astype(BF)

    return called(
        body,
        jax.ShapeDtypeStruct((rows, features + 128), BF),
        2 * rows * lines * features,
        grid=(1,),
        in_specs=[
            pl.BlockSpec(memory_space=pltpu.SMEM),
            pl.BlockSpec((lines, features), lambda i: (0, steps)),
            pl.BlockSpec((lines, 128), lambda i: (0, (steps + 1) * features // 128)),
        ],
        out_specs=whole((rows, features + 128)),
    )(masks, third, third)


def pool_gradient(third, asked, pool_hidden, inverse, norm_gain):
    lines, width = third.shape
    pool, features = pool_hidden.shape
    steps = asked.shape[0]
    tile = 256

    def body(third_ref, asked_ref, hidden_ref, inverse_ref, gain_ref, out_ref):
        row = sublanes_of((tile, lines)) + pl.program_id(0) * tile
        delta = jnp.zeros((tile, features), F32)
        value = jnp.zeros((tile, 1), F32)
        lane = lanes_of((tile, 128))
        for t in range(steps):
            back = hot(row == asked_ref[t : t + 1, :])
            delta = delta + dot(back, third_ref[:, t * features : (t + 1) * features])
            terms = dot(back, third_ref[:, width - 128 :])
            mine = (lane >= 3 * t) & (lane < 3 * t + 3)
            value = value + jnp.sum(jnp.where(mine, terms, 0.0), axis=1, keepdims=True)
        gain = gain_ref[...]
        scaled = gain * hidden_ref[...].astype(F32)
        inner = delta - scaled * (inverse_ref[...] * value)
        out_ref[...] = (gain * inverse_ref[...] * inner).astype(BF)

    tiled = lambda n: pl.BlockSpec((tile, n), lambda i: (i, 0))
    return called(
        body,
        jax.ShapeDtypeStruct((pool, features), BF),
        2 * pool * lines * steps * features,
        grid=(pool // tile,),
        in_specs=[
            whole((lines, width)),
            whole((steps, lines)),
            tiled(features),
            tiled(1),
            whole((1, features)),
        ],
        out_specs=tiled(features),
    )(third, asked, pool_hidden, inverse[:, None], norm_gain[None, :])


def per_device(
    query_hidden, positive_hidden, pool_hidden, norm_gain, hard_ids, location, partner_masks
):
    devices = lax.axis_size("batch")
    parts = lax.axis_size("mp")
    me_mp = lax.axis_index("mp")
    rows_dev, feature_dev = query_hidden.shape
    pool_dev = pool_hidden.shape[0]
    hard_count = hard_ids.shape[0] * hard_ids.shape[1]
    capacity = max(hard_count // 32, 2 * ((hard_count + devices - 1) // devices))
    steps = (capacity + GROUP - 1) // GROUP
    chunk = rows_dev // devices
    lines = devices * GROUP
    share = rows_dev // parts
    int_range = lambda n: jnp.arange(n, dtype=jnp.int32)

    partial_squares = jnp.concatenate(
        [row_squares(x, norm_gain) for x in (positive_hidden, query_hidden, pool_hidden)]
    )
    inverse = lax.rsqrt(summed(partial_squares) + EPSILON)
    inverse_p, inverse_q, inverse_pool = jnp.split(inverse, [rows_dev, 2 * rows_dev])
    emb_p = embedding(positive_hidden, norm_gain, inverse_p)

    ids = after(hard_ids, partial_squares).T.reshape(-1)
    storage = looked_up(location, ids)
    owners = storage // pool_dev
    local_row = storage % pool_dev
    order = int_range(hard_count)
    earlier = (owners[:, None] == owners[None, :]) & (order[None, :] < order[:, None])
    slot_index = jnp.sum(earlier.astype(jnp.int32), axis=1)
    line = slot_index % GROUP
    group = slot_index // GROUP
    code = group * lines + owners * GROUP + line
    lane = group * (GROUP // chunk) + line // chunk
    lanes = int_range(128)[None, :]
    wanted = local_row + 1
    digits = jnp.where(
        lanes == lane[:, None],
        (wanted >> 4)[:, None],
        jnp.where(lanes == lane[:, None] + 64, (wanted & 15)[:, None], 0),
    ).astype(BF)
    request_line = one_hot(owners * chunk + line % chunk, devices * chunk)
    requests = dot(request_line, digits, ((0,), (0,))).astype(BF)

    first = exchanged(
        jnp.concatenate(
            [
                emb_p.reshape(devices, chunk, feature_dev),
                requests.reshape(devices, chunk, 128),
            ],
            axis=2,
        )
    ).reshape(rows_dev, feature_dev + 128)
    halves = GROUP // chunk
    asked = first[:, feature_dev:].reshape(devices, chunk, 128).astype(jnp.int32)
    asked = asked[:, :, : steps * halves] * 16 + asked[:, :, 64 : 64 + steps * halves] - 1
    asked = asked.reshape(devices, chunk, steps, halves).transpose(2, 0, 3, 1).reshape(steps, lines)

    emb_q = embedding(query_hidden, norm_gain, inverse_q)
    emb_pool = embedding(pool_hidden, norm_gain, inverse_pool)
    turned_q = lax.dynamic_slice_in_dim(
        jnp.concatenate([emb_q, emb_q], axis=0), me_mp * share, rows_dev
    )

    arrived = exchanged(served_rows(first, emb_pool, partner_masks, steps, chunk))

    own_parts = dot(turned_q, emb_p, ((1,), (1,)))
    scores_own = own_parts[:share]
    for step in range(1, parts):
        scores_own = scores_own + lax.ppermute(
            own_parts[step * share : (step + 1) * share],
            "mp",
            [(i, (i + step) % parts) for i in range(parts)],
        )
    scores_own = scores_own / SOFTMAX_TEMPER
    hard_emb, kept, *coded = partial_scores(turned_q, arrived, code, steps, parts)
    total = jnp.zeros_like(kept)
    for step in range(1, parts):
        total = total + lax.ppermute(
            coded[step - 1], "mp", [(i, (i + step) % parts) for i in range(parts)]
        ).astype(F32)
    scores_far = (kept + total * (1.0 / FIXED)) * (1.0 / SOFTMAX_TEMPER)
    exp_own = jnp.exp(scores_own)
    exp_far = jnp.exp(scores_far)
    sums = jnp.sum(exp_own, axis=1) + jnp.sum(exp_far, axis=1)
    own = int_range(share)[:, None] + me_mp * share == int_range(rows_dev)[None, :]
    losses = jnp.log(sums) - jnp.sum(jnp.where(own, scores_own, 0.0), axis=1)
    ratio = 1.0 / sums
    weights_own = ((exp_own * ratio[:, None] - own.astype(F32)) * SCALE).astype(BF)
    weights_far = (exp_far * ratio[:, None] * SCALE).astype(BF)

    def gathered(piece):
        pieces = [piece]
        for step in range(1, parts):
            pieces.append(
                lax.ppermute(piece, "mp", [((i + step) % parts, i) for i in range(parts)])
            )
        return pieces

    values = summed(
        jnp.concatenate(
            [
                jnp.sum(weights_far.astype(F32) * scores_far, axis=0),
                jnp.sum(weights_own.astype(F32) * scores_own, axis=0),
            ]
        )
        * SOFTMAX_TEMPER
    )
    far_pieces = gathered(weights_far)
    columns = lines + hard_count
    third = exchanged(
        outgoing_rows(far_pieces, code, values[:columns], turned_q, lines, steps)
    )
    weights_own = jnp.concatenate(gathered(weights_own), axis=0)
    weights_far = jnp.concatenate(far_pieces, axis=0)

    def natural(x):
        return lax.dynamic_slice_in_dim(
            jnp.concatenate([x, x], axis=0), (parts - me_mp) * share, rows_dev
        )

    def row_products(hidden, delta):
        return summed(jnp.sum(scaled_rows(hidden, norm_gain) * delta, axis=1))

    delta_q = natural(
        dot(weights_own, emb_p)
        + dot(weights_far[:, :lines], arrived[:, steps * feature_dev :])
        + dot(weights_far[:, lines:], hard_emb)
    )
    product_q = summed(jnp.sum(scaled_rows(query_hidden, norm_gain) * delta_q, axis=1))
    grad_q = gradient(query_hidden, inverse_q, delta_q, product_q, norm_gain)
    delta_own = dot(weights_own, turned_q, ((0,), (0,)))

    masks = after(after(partner_masks, grad_q), delta_own)
    merged = merged_rows(third, masks, rows_dev, feature_dev, steps, chunk)
    home = exchanged(merged)
    grad_pool = pool_gradient(third, asked, pool_hidden, inverse_pool, norm_gain)
    home = home.astype(F32)
    delta_p = delta_own + home[:, :feature_dev]
    value_p = values[columns:] + jnp.sum(home[:, feature_dev : feature_dev + 3], axis=1)
    grad_p = gradient(positive_hidden, inverse_p, delta_p, value_p / inverse_p, norm_gain)
    return (losses, grad_q, grad_p, grad_pool)


def solution(mesh):
    placed = (
        P("batch", "mp"),
        P("batch", "mp"),
        P("batch", "mp"),
        P("mp"),
        P("batch", None),
        P(),
        P(),
    )
    return jax.shard_map(
        per_device,
        mesh=mesh,
        in_specs=placed,
        out_specs=(P(("batch", "mp")), P("batch", "mp"), P("batch", "mp"), P("batch", "mp")),
        check_vma=False,
    )
```

```python
import jax
import jax.numpy as jnp
from jax import lax
from jax.experimental import pallas as pl
from jax.experimental.pallas import tpu as pltpu
from jax.sharding import PartitionSpec as P

MODEL_WIDTH = 4096
SOFTMAX_TEMPER = 0.02
EPSILON = 1e-06
FIXED = 32000.0
SCALE = MODEL_WIDTH / 64.0 / SOFTMAX_TEMPER
BF = jnp.bfloat16
F32 = jnp.float32


def exchanged(x):
    return lax.all_to_all(x, "batch", split_axis=0, concat_axis=0, tiled=True)


def scaled_rows(hidden, norm_gain):
    return norm_gain[None, :] * hidden.astype(F32)


def row_squares(hidden, norm_gain):
    scaled = scaled_rows(hidden, norm_gain)
    return jnp.sum(scaled * scaled, axis=1)


def embedding(hidden, norm_gain, inverse):
    return (scaled_rows(hidden, norm_gain) * inverse[:, None]).astype(BF)


def gradient(hidden, inverse, delta, product, norm_gain):
    inner = delta - scaled_rows(hidden, norm_gain) * (inverse * inverse * product)[:, None]
    return (norm_gain[None, :] * inverse[:, None] * inner).astype(BF)


def dot(a, b, dims=((1,), (0,))):
    return lax.dot_general(a, b, (dims, ((), ())), preferred_element_type=F32)


def one_hot(column, width):
    return (column[:, None] == jnp.arange(width, dtype=jnp.int32)[None, :]).astype(BF)


def looked_up(table, ids):
    rows = table.shape[0] // 128
    bytes_of = table.reshape(rows, 128)
    parts = jnp.concatenate([bytes_of >> 8, bytes_of & 255], axis=1).astype(BF)
    found = dot(one_hot(ids >> 7, rows), parts)
    value = found[:, :128] * 256.0 + found[:, 128:]
    lane = (ids & 127)[:, None] == jnp.arange(128, dtype=jnp.int32)[None, :]
    return jnp.sum(jnp.where(lane, value, 0.0), axis=1).astype(jnp.int32)


def after(x, value):
    return jnp.where(jnp.isnan(value.reshape(-1)[0].astype(F32)), jnp.zeros_like(x), x)


def summed(x):
    parts = lax.axis_size("mp")
    total = x
    for step in range(1, parts):
        total = total + lax.ppermute(x, "mp", [(i, (i + step) % parts) for i in range(parts)])
    return total


VMEM_BYTES = 40 * 1024 * 1024
GROUP = 8


def called(body, out_shape, flops, **more):
    return pl.pallas_call(
        body,
        out_shape=out_shape,
        compiler_params=pltpu.CompilerParams(vmem_limit_bytes=VMEM_BYTES),
        cost_estimate=pl.CostEstimate(flops=flops, bytes_accessed=8 << 20, transcendentals=0),
        **more,
    )


def lanes_of(shape):
    return lax.broadcasted_iota(jnp.int32, shape, 1)


def sublanes_of(shape):
    return lax.broadcasted_iota(jnp.int32, shape, 0)


def hot(matches):
    return matches.astype(F32).astype(BF)


def whole(shape):
    return pl.BlockSpec(shape, lambda i: (0,) * len(shape))


def split_value(value, lane, at):
    high = value.astype(BF).astype(F32)
    middle = (value - high).astype(BF).astype(F32)
    low = value - high - middle
    return jnp.where(
        lane == at, high, jnp.where(lane == at + 1, middle, jnp.where(lane == at + 2, low, 0.0))
    )


def served_rows(first, emb_pool, masks, steps, chunk):
    rows, width = first.shape
    pool, features = emb_pool.shape
    lines = rows // chunk * GROUP
    halves = GROUP // chunk

    def body(masks_ref, first_ref, pool_ref, out_ref, digits_ref):
        step = pl.program_id(0)
        line = sublanes_of((lines, 1))
        receiver = line // GROUP
        part = (line % GROUP) // chunk
        piece = line % chunk

        @pl.when(step == 0)
        def _():
            spreading = hot(lanes_of((lines, rows)) == receiver * chunk + piece)
            digits_ref[...] = dot(spreading, first_ref[:, features:])

        @pl.when(step < steps)
        def _():
            digits = digits_ref[...]
            lane = lanes_of(digits.shape)
            place = step * halves + part
            value = jnp.where(lane == place, digits * 16.0, 0.0)
            value = jnp.where(lane == place + 64, digits, value)
            asked = jnp.sum(value, axis=1, keepdims=True).astype(jnp.int32) - 1
            out_ref[...] = dot(hot(lanes_of((lines, pool)) == asked), pool_ref[...]).astype(BF)

        @pl.when(step == steps)
        def _():
            mask = jnp.where(part == 0, masks_ref[0], masks_ref[1])
            source = (receiver ^ mask) * chunk + piece
            chosen = hot(lanes_of((lines, rows)) == source)
            out_ref[...] = dot(chosen, first_ref[:, :features]).astype(BF)

    return called(
        body,
        pltpu.HBM((lines, (steps + 1) * features), BF),
        2 * lines * steps * pool * features,
        grid=(steps + 1,),
        in_specs=[
            pl.BlockSpec(memory_space=pltpu.SMEM),
            whole((rows, width)),
            whole((pool, features)),
        ],
        out_specs=pl.BlockSpec((lines, features), lambda i: (0, i)),
        scratch_shapes=[pltpu.VMEM((lines, 128), F32)],
    )(masks, first, emb_pool)


def partial_scores(turned_q, arrived, code, steps, parts):
    rows, features = turned_q.shape
    lines = arrived.shape[0]
    hard = code.shape[0]
    share = rows // parts

    def body(q_ref, arrived_ref, code_ref, kept_ref, *rest):
        *coded_refs, total_ref = rest
        step = pl.program_id(0)

        def score(candidates, at):
            count = candidates.shape[0]
            partial = dot(q_ref[...], candidates, ((1,), (1,)))
            kept_ref[:, at : at + count] = partial[:share]
            for i, ref in enumerate(coded_refs):
                coded = jnp.round(partial[(i + 1) * share : (i + 2) * share] * FIXED)
                ref[:, at : at + count] = coded.astype(jnp.int32).astype(jnp.int16)

        @pl.when(step == 0)
        def _():
            score(arrived_ref[...], 0)
            total_ref[...] = jnp.zeros_like(total_ref)

        @pl.when(step > 0)
        def _():
            chosen = hot(lanes_of((hard, lines)) + (step - 1) * lines == code_ref[...])
            total_ref[...] += dot(chosen, arrived_ref[...])

        @pl.when(step == steps)
        def _():
            score(total_ref[...].astype(BF), lines)

    columns = lines + hard
    return called(
        body,
        [jax.ShapeDtypeStruct((share, columns), F32)]
        + [jax.ShapeDtypeStruct((share, columns), jnp.int16)] * (parts - 1),
        2 * hard * steps * lines * features,
        grid=(steps + 1,),
        in_specs=[
            whole((rows, features)),
            pl.BlockSpec((lines, features), lambda i: (0, (i + steps) % (steps + 1))),
            whole((hard, 1)),
        ],
        out_specs=[whole((share, columns))] * parts,
        scratch_shapes=[pltpu.VMEM((hard, features), F32)],
    )(turned_q, arrived, code[:, None])


def outgoing_rows(pieces, code, values, turned_q, lines, steps):
    share, columns = pieces[0].shape
    rows, features = turned_q.shape
    hard = code.shape[0]
    tile = lines // 2

    def body(*refs):
        code_ref, near_ref, far_ref, q_ref, out_ref, all_ref = refs[len(pieces) :]
        step = pl.program_id(0)

        @pl.when(step == 0)
        def _():
            for i, ref in enumerate(refs[: len(pieces)]):
                all_ref[i * share : (i + 1) * share, :] = ref[...]

        lane = lanes_of((tile, 128))
        line = sublanes_of((tile, hard)) + step * tile
        extra = jnp.zeros((tile, 128), F32)
        for t in range(steps):
            matches = line + t * lines == code_ref[...]
            value = jnp.sum(jnp.where(matches, far_ref[...], 0.0), axis=1, keepdims=True)
            extra = extra + split_value(value, lane, 3 * t)
            weights = dot(hot(matches), all_ref[:, lines:], ((1,), (1,))).astype(BF)
            out_ref[:, t * features : (t + 1) * features] = dot(weights, q_ref[...]).astype(BF)
        near = sublanes_of((tile, lines)) + step * tile == lanes_of((tile, lines))
        value = jnp.sum(jnp.where(near, near_ref[...], 0.0), axis=1, keepdims=True)
        extra = extra + split_value(value, lane, 3 * steps)
        weights = all_ref[:, pl.ds(pl.multiple_of(step * tile, tile), tile)]
        delta = dot(weights, q_ref[...], ((0,), (0,)))
        out_ref[:, steps * features : (steps + 1) * features] = delta.astype(BF)
        out_ref[:, (steps + 1) * features :] = extra.astype(BF)

    width = (steps + 1) * features + 128
    return called(
        body,
        pltpu.HBM((lines, width), BF),
        2 * lines * (steps + 1) * rows * (hard + features),
        grid=(2,),
        in_specs=[whole((share, columns))] * len(pieces)
        + [whole((1, hard)), whole((1, lines)), whole((1, hard)), whole((rows, features))],
        out_specs=pl.BlockSpec((tile, width), lambda i: (i, 0)),
        scratch_shapes=[pltpu.VMEM((rows, columns), BF)],
    )(
        *pieces,
        code[None, :],
        values[None, :lines],
        values[None, lines:],
        turned_q,
    )


def merged_rows(third, masks, rows, features, steps, chunk):
    lines, width = third.shape

    def body(masks_ref, near_ref, extra_ref, out_ref):
        line = lanes_of((1, lines))
        mask = jnp.where((line % GROUP) // chunk == 0, masks_ref[0], masks_ref[1])
        target = ((line // GROUP) ^ mask) * chunk + line % chunk
        back = hot(sublanes_of((rows, lines)) == target)
        out_ref[:, :features] = dot(back, near_ref[...]).astype(BF)
        lane = lanes_of((rows, 128))
        terms = dot(back, extra_ref[...])
        mine = (lane >= 3 * steps) & (lane < 3 * steps + 3)
        value = jnp.sum(jnp.where(mine, terms, 0.0), axis=1, keepdims=True)
        out_ref[:, features:] = split_value(value, lane, 0).astype(BF)

    return called(
        body,
        jax.ShapeDtypeStruct((rows, features + 128), BF),
        2 * rows * lines * features,
        grid=(1,),
        in_specs=[
            pl.BlockSpec(memory_space=pltpu.SMEM),
            pl.BlockSpec((lines, features), lambda i: (0, steps)),
            pl.BlockSpec((lines, 128), lambda i: (0, (steps + 1) * features // 128)),
        ],
        out_specs=whole((rows, features + 128)),
    )(masks, third, third)


def pool_gradient(third, asked, pool_hidden, inverse, norm_gain):
    lines, width = third.shape
    pool, features = pool_hidden.shape
    steps = asked.shape[0]
    tile = 256

    def body(third_ref, asked_ref, hidden_ref, inverse_ref, gain_ref, out_ref):
        row = sublanes_of((tile, lines)) + pl.program_id(0) * tile
        delta = jnp.zeros((tile, features), F32)
        value = jnp.zeros((tile, 1), F32)
        lane = lanes_of((tile, 128))
        for t in range(steps):
            back = hot(row == asked_ref[t : t + 1, :])
            delta = delta + dot(back, third_ref[:, t * features : (t + 1) * features])
            terms = dot(back, third_ref[:, width - 128 :])
            mine = (lane >= 3 * t) & (lane < 3 * t + 3)
            value = value + jnp.sum(jnp.where(mine, terms, 0.0), axis=1, keepdims=True)
        gain = gain_ref[...]
        scaled = gain * hidden_ref[...].astype(F32)
        inner = delta - scaled * (inverse_ref[...] * value)
        out_ref[...] = (gain * inverse_ref[...] * inner).astype(BF)

    tiled = lambda n: pl.BlockSpec((tile, n), lambda i: (i, 0))
    return called(
        body,
        jax.ShapeDtypeStruct((pool, features), BF),
        2 * pool * lines * steps * features,
        grid=(pool // tile,),
        in_specs=[
            whole((lines, width)),
            whole((steps, lines)),
            tiled(features),
            tiled(1),
            whole((1, features)),
        ],
        out_specs=tiled(features),
    )(third, asked, pool_hidden, inverse[:, None], norm_gain[None, :])


def per_device(
    query_hidden, positive_hidden, pool_hidden, norm_gain, hard_ids, location, partner_masks
):
    devices = lax.axis_size("batch")
    parts = lax.axis_size("mp")
    me_mp = lax.axis_index("mp")
    rows_dev, feature_dev = query_hidden.shape
    pool_dev = pool_hidden.shape[0]
    hard_count = hard_ids.shape[0] * hard_ids.shape[1]
    capacity = max(hard_count // 32, 2 * ((hard_count + devices - 1) // devices))
    steps = (capacity + GROUP - 1) // GROUP
    chunk = rows_dev // devices
    lines = devices * GROUP
    share = rows_dev // parts
    int_range = lambda n: jnp.arange(n, dtype=jnp.int32)

    partial_squares = jnp.concatenate(
        [row_squares(x, norm_gain) for x in (positive_hidden, query_hidden, pool_hidden)]
    )
    inverse = lax.rsqrt(summed(partial_squares) + EPSILON)
    inverse_p, inverse_q, inverse_pool = jnp.split(inverse, [rows_dev, 2 * rows_dev])
    emb_p = embedding(positive_hidden, norm_gain, inverse_p)

    ids = after(hard_ids, partial_squares).T.reshape(-1)
    storage = looked_up(location, ids)
    owners = storage // pool_dev
    local_row = storage % pool_dev
    order = int_range(hard_count)
    earlier = (owners[:, None] == owners[None, :]) & (order[None, :] < order[:, None])
    slot_index = jnp.sum(earlier.astype(jnp.int32), axis=1)
    line = slot_index % GROUP
    group = slot_index // GROUP
    code = group * lines + owners * GROUP + line
    lane = group * (GROUP // chunk) + line // chunk
    lanes = int_range(128)[None, :]
    wanted = local_row + 1
    digits = jnp.where(
        lanes == lane[:, None],
        (wanted >> 4)[:, None],
        jnp.where(lanes == lane[:, None] + 64, (wanted & 15)[:, None], 0),
    ).astype(BF)
    request_line = one_hot(owners * chunk + line % chunk, devices * chunk)
    requests = dot(request_line, digits, ((0,), (0,))).astype(BF)

    first = exchanged(
        jnp.concatenate(
            [
                emb_p.reshape(devices, chunk, feature_dev),
                requests.reshape(devices, chunk, 128),
            ],
            axis=2,
        )
    ).reshape(rows_dev, feature_dev + 128)
    halves = GROUP // chunk
    asked = first[:, feature_dev:].reshape(devices, chunk, 128).astype(jnp.int32)
    asked = asked[:, :, : steps * halves] * 16 + asked[:, :, 64 : 64 + steps * halves] - 1
    asked = asked.reshape(devices, chunk, steps, halves).transpose(2, 0, 3, 1).reshape(steps, lines)

    emb_p = embedding(positive_hidden, norm_gain, after(inverse_p, first))
    emb_q = embedding(query_hidden, norm_gain, inverse_q)
    emb_pool = embedding(pool_hidden, norm_gain, inverse_pool)
    turned_q = lax.dynamic_slice_in_dim(
        jnp.concatenate([emb_q, emb_q], axis=0), me_mp * share, rows_dev
    )

    arrived = exchanged(served_rows(first, emb_pool, partner_masks, steps, chunk))

    own_parts = dot(turned_q, emb_p, ((1,), (1,)))
    scores_own = own_parts[:share]
    for step in range(1, parts):
        scores_own = scores_own + lax.ppermute(
            own_parts[step * share : (step + 1) * share],
            "mp",
            [(i, (i + step) % parts) for i in range(parts)],
        )
    scores_own = scores_own / SOFTMAX_TEMPER
    kept, *coded = partial_scores(turned_q, arrived, code, steps, parts)
    total = jnp.zeros_like(kept)
    for step in range(1, parts):
        total = total + lax.ppermute(
            coded[step - 1], "mp", [(i, (i + step) % parts) for i in range(parts)]
        ).astype(F32)
    scores_far = (kept + total * (1.0 / FIXED)) * (1.0 / SOFTMAX_TEMPER)
    exp_own = jnp.exp(scores_own)
    exp_far = jnp.exp(scores_far)
    sums = jnp.sum(exp_own, axis=1) + jnp.sum(exp_far, axis=1)
    own = int_range(share)[:, None] + me_mp * share == int_range(rows_dev)[None, :]
    losses = jnp.log(sums) - jnp.sum(jnp.where(own, scores_own, 0.0), axis=1)
    ratio = 1.0 / sums
    weights_own = ((exp_own * ratio[:, None] - own.astype(F32)) * SCALE).astype(BF)
    weights_far = (exp_far * ratio[:, None] * SCALE).astype(BF)

    def gathered(piece):
        pieces = [piece]
        for step in range(1, parts):
            pieces.append(
                lax.ppermute(piece, "mp", [((i + step) % parts, i) for i in range(parts)])
            )
        return pieces

    far_pieces = gathered(weights_far)
    values = summed(
        jnp.concatenate(
            [
                jnp.sum(weights_far.astype(F32) * scores_far, axis=0),
                jnp.sum(weights_own.astype(F32) * scores_own, axis=0),
            ]
        )
        * SOFTMAX_TEMPER
    )
    columns = lines + hard_count
    third = exchanged(
        outgoing_rows(far_pieces, code, values[:columns], turned_q, lines, steps)
    )
    weights_own = jnp.concatenate(gathered(weights_own), axis=0)
    weights_far = jnp.concatenate(far_pieces, axis=0)

    def natural(x):
        return lax.dynamic_slice_in_dim(
            jnp.concatenate([x, x], axis=0), (parts - me_mp) * share, rows_dev
        )

    def row_products(hidden, delta):
        return summed(jnp.sum(scaled_rows(hidden, norm_gain) * delta, axis=1))

    weights_slots = dot(weights_far[:, lines:], one_hot(code, steps * lines)).astype(BF)
    weights_slots = jnp.concatenate([weights_slots, weights_far[:, :lines]], axis=1)
    delta_q = dot(weights_own, emb_p)
    for t in range(steps + 1):
        delta_q = delta_q + dot(
            weights_slots[:, t * lines : (t + 1) * lines],
            arrived[:, t * feature_dev : (t + 1) * feature_dev],
        )
    delta_q = natural(delta_q)
    product_q = summed(jnp.sum(scaled_rows(query_hidden, norm_gain) * delta_q, axis=1))
    grad_q = gradient(query_hidden, inverse_q, delta_q, product_q, norm_gain)
    delta_own = dot(weights_own, turned_q, ((0,), (0,)))

    masks = after(after(partner_masks, grad_q), delta_own)
    merged = merged_rows(third, masks, rows_dev, feature_dev, steps, chunk)
    home = exchanged(merged)
    grad_pool = pool_gradient(third, asked, pool_hidden, inverse_pool, norm_gain)
    home = home.astype(F32)
    delta_p = delta_own + home[:, :feature_dev]
    value_p = values[columns:] + jnp.sum(home[:, feature_dev : feature_dev + 3], axis=1)
    grad_p = gradient(positive_hidden, inverse_p, delta_p, value_p / inverse_p, norm_gain)
    return (losses, grad_q, grad_p, grad_pool)


def solution(mesh):
    placed = (
        P("batch", "mp"),
        P("batch", "mp"),
        P("batch", "mp"),
        P("mp"),
        P("batch", None),
        P(),
        P(),
    )
    return jax.shard_map(
        per_device,
        mesh=mesh,
        in_specs=placed,
        out_specs=(P(("batch", "mp")), P("batch", "mp"), P("batch", "mp"), P("batch", "mp")),
        check_vma=False,
    )
```

```python
import jax
import jax.numpy as jnp
from jax import lax
from jax.experimental import pallas as pl
from jax.experimental.pallas import tpu as pltpu
from jax.sharding import PartitionSpec as P

MODEL_WIDTH = 4096
SOFTMAX_TEMPER = 0.02
EPSILON = 1e-06
FIXED = 32000.0
SCALE = MODEL_WIDTH / 64.0 / SOFTMAX_TEMPER
BF = jnp.bfloat16
F32 = jnp.float32


def exchanged(x):
    return lax.all_to_all(x, "batch", split_axis=0, concat_axis=0, tiled=True)


def scaled_rows(hidden, norm_gain):
    return norm_gain[None, :] * hidden.astype(F32)


def row_squares(hidden, norm_gain):
    scaled = scaled_rows(hidden, norm_gain)
    return jnp.sum(scaled * scaled, axis=1)


def embedding(hidden, norm_gain, inverse):
    return (scaled_rows(hidden, norm_gain) * inverse[:, None]).astype(BF)


def gradient(hidden, inverse, delta, product, norm_gain):
    inner = delta - scaled_rows(hidden, norm_gain) * (inverse * inverse * product)[:, None]
    return (norm_gain[None, :] * inverse[:, None] * inner).astype(BF)


def dot(a, b, dims=((1,), (0,))):
    return lax.dot_general(a, b, (dims, ((), ())), preferred_element_type=F32)


def one_hot(column, width):
    return (column[:, None] == jnp.arange(width, dtype=jnp.int32)[None, :]).astype(BF)


def looked_up(table, ids):
    rows = table.shape[0] // 128
    bytes_of = table.reshape(rows, 128)
    parts = jnp.concatenate([bytes_of >> 8, bytes_of & 255], axis=1).astype(BF)
    found = dot(one_hot(ids >> 7, rows), parts)
    value = found[:, :128] * 256.0 + found[:, 128:]
    lane = (ids & 127)[:, None] == jnp.arange(128, dtype=jnp.int32)[None, :]
    return jnp.sum(jnp.where(lane, value, 0.0), axis=1).astype(jnp.int32)


def after(x, value):
    corner = lax.slice(value, (0,) * value.ndim, (1,) * value.ndim).astype(F32)
    return jnp.where(jnp.isnan(corner).reshape((1,) * x.ndim), jnp.zeros_like(x), x)


def folded(x):
    parts = lax.axis_size("mp")
    for bit in range(parts.bit_length() - 1):
        x = x + lax.ppermute(x, "mp", [(i, i ^ 1 << bit) for i in range(parts)])
    return x


def summed(x):
    parts = lax.axis_size("mp")
    total = x
    for step in range(1, parts):
        total = total + lax.ppermute(x, "mp", [(i, (i + step) % parts) for i in range(parts)])
    return total


VMEM_BYTES = 40 * 1024 * 1024
GROUP = 8


def called(body, out_shape, flops, **more):
    return pl.pallas_call(
        body,
        out_shape=out_shape,
        compiler_params=pltpu.CompilerParams(vmem_limit_bytes=VMEM_BYTES),
        cost_estimate=pl.CostEstimate(flops=flops, bytes_accessed=8 << 20, transcendentals=0),
        **more,
    )


def lanes_of(shape):
    return lax.broadcasted_iota(jnp.int32, shape, 1)


def sublanes_of(shape):
    return lax.broadcasted_iota(jnp.int32, shape, 0)


def hot(matches):
    return matches.astype(F32).astype(BF)


def whole(shape):
    return pl.BlockSpec(shape, lambda i: (0,) * len(shape))


def split_value(value, lane, at):
    high = value.astype(BF).astype(F32)
    middle = (value - high).astype(BF).astype(F32)
    low = value - high - middle
    return jnp.where(
        lane == at, high, jnp.where(lane == at + 1, middle, jnp.where(lane == at + 2, low, 0.0))
    )


def served_rows(first, emb_pool, masks, steps, chunk):
    rows, width = first.shape
    pool, features = emb_pool.shape
    lines = rows // chunk * GROUP
    halves = GROUP // chunk

    def body(masks_ref, first_ref, pool_ref, out_ref, digits_ref):
        step = pl.program_id(0)
        line = sublanes_of((lines, 1))
        receiver = line // GROUP
        part = (line % GROUP) // chunk
        piece = line % chunk

        @pl.when(step == 0)
        def _():
            spreading = hot(lanes_of((lines, rows)) == receiver * chunk + piece)
            digits_ref[...] = dot(spreading, first_ref[:, features:])

        @pl.when(step < steps)
        def _():
            digits = digits_ref[...]
            lane = lanes_of(digits.shape)
            place = step * halves + part
            value = jnp.where(lane == place, digits * 16.0, 0.0)
            value = jnp.where(lane == place + 64, digits, value)
            asked = jnp.sum(value, axis=1, keepdims=True).astype(jnp.int32) - 1
            out_ref[...] = dot(hot(lanes_of((lines, pool)) == asked), pool_ref[...]).astype(BF)

        @pl.when(step == steps)
        def _():
            mask = jnp.where(part == 0, masks_ref[0], masks_ref[1])
            source = (receiver ^ mask) * chunk + piece
            chosen = hot(lanes_of((lines, rows)) == source)
            out_ref[...] = dot(chosen, first_ref[:, :features]).astype(BF)

    return called(
        body,
        pltpu.HBM((lines, (steps + 1) * features), BF),
        2 * lines * steps * pool * features,
        grid=(steps + 1,),
        in_specs=[
            pl.BlockSpec(memory_space=pltpu.SMEM),
            whole((rows, width)),
            whole((pool, features)),
        ],
        out_specs=pl.BlockSpec((lines, features), lambda i: (0, i)),
        scratch_shapes=[pltpu.VMEM((lines, 128), F32)],
    )(masks, first, emb_pool)


def partial_scores(turned_q, arrived, code, steps, parts):
    rows, features = turned_q.shape
    lines = arrived.shape[0]
    hard = code.shape[0]
    share = rows // parts

    def body(q_ref, arrived_ref, code_ref, kept_ref, *rest):
        *coded_refs, total_ref = rest
        step = pl.program_id(0)

        def score(candidates, at):
            count = candidates.shape[0]
            partial = dot(q_ref[...], candidates, ((1,), (1,)))
            kept_ref[:, at : at + count] = partial[:share]
            for i, ref in enumerate(coded_refs):
                coded = jnp.round(partial[(i + 1) * share : (i + 2) * share] * FIXED)
                ref[:, at : at + count] = coded.astype(jnp.int32).astype(jnp.int16)

        @pl.when(step == 0)
        def _():
            score(arrived_ref[...], 0)
            total_ref[...] = jnp.zeros_like(total_ref)

        @pl.when(step > 0)
        def _():
            chosen = hot(lanes_of((hard, lines)) + (step - 1) * lines == code_ref[...])
            total_ref[...] += dot(chosen, arrived_ref[...])

        @pl.when(step == steps)
        def _():
            score(total_ref[...].astype(BF), lines)

    columns = lines + hard
    return called(
        body,
        [jax.ShapeDtypeStruct((share, columns), F32)]
        + [jax.ShapeDtypeStruct((share, columns), jnp.int16)] * (parts - 1),
        2 * hard * steps * lines * features,
        grid=(steps + 1,),
        in_specs=[
            whole((rows, features)),
            pl.BlockSpec((lines, features), lambda i: (0, (i + steps) % (steps + 1))),
            whole((hard, 1)),
        ],
        out_specs=[whole((share, columns))] * parts,
        scratch_shapes=[pltpu.VMEM((hard, features), F32)],
    )(turned_q, arrived, code[:, None])


def outgoing_rows(pieces, code, values, turned_q, lines, steps):
    share, columns = pieces[0].shape
    rows, features = turned_q.shape
    hard = code.shape[0]
    tile = lines // 2

    def body(*refs):
        code_ref, near_ref, far_ref, q_ref, out_ref, all_ref = refs[len(pieces) :]
        step = pl.program_id(0)

        @pl.when(step == 0)
        def _():
            for i, ref in enumerate(refs[: len(pieces)]):
                all_ref[i * share : (i + 1) * share, :] = ref[...]

        lane = lanes_of((tile, 128))
        line = sublanes_of((tile, hard)) + step * tile
        extra = jnp.zeros((tile, 128), F32)
        for t in range(steps):
            matches = line + t * lines == code_ref[...]
            value = jnp.sum(jnp.where(matches, far_ref[...], 0.0), axis=1, keepdims=True)
            extra = extra + split_value(value, lane, 3 * t)
            weights = dot(hot(matches), all_ref[:, lines:], ((1,), (1,))).astype(BF)
            out_ref[:, t * features : (t + 1) * features] = dot(weights, q_ref[...]).astype(BF)
        near = sublanes_of((tile, lines)) + step * tile == lanes_of((tile, lines))
        value = jnp.sum(jnp.where(near, near_ref[...], 0.0), axis=1, keepdims=True)
        extra = extra + split_value(value, lane, 3 * steps)
        weights = all_ref[:, pl.ds(pl.multiple_of(step * tile, tile), tile)]
        delta = dot(weights, q_ref[...], ((0,), (0,)))
        out_ref[:, steps * features : (steps + 1) * features] = delta.astype(BF)
        out_ref[:, (steps + 1) * features :] = extra.astype(BF)

    width = (steps + 1) * features + 128
    return called(
        body,
        pltpu.HBM((lines, width), BF),
        2 * lines * (steps + 1) * rows * (hard + features),
        grid=(2,),
        in_specs=[whole((share, columns))] * len(pieces)
        + [whole((1, hard)), whole((1, lines)), whole((1, hard)), whole((rows, features))],
        out_specs=pl.BlockSpec((tile, width), lambda i: (i, 0)),
        scratch_shapes=[pltpu.VMEM((rows, columns), BF)],
    )(
        *pieces,
        code[None, :],
        values[None, :lines],
        values[None, lines:],
        turned_q,
    )


def merged_rows(third, masks, rows, features, steps, chunk):
    lines, width = third.shape

    def body(masks_ref, near_ref, extra_ref, out_ref):
        line = lanes_of((1, lines))
        mask = jnp.where((line % GROUP) // chunk == 0, masks_ref[0], masks_ref[1])
        target = ((line // GROUP) ^ mask) * chunk + line % chunk
        back = hot(sublanes_of((rows, lines)) == target)
        out_ref[:, :features] = dot(back, near_ref[...]).astype(BF)
        lane = lanes_of((rows, 128))
        terms = dot(back, extra_ref[...])
        mine = (lane >= 3 * steps) & (lane < 3 * steps + 3)
        value = jnp.sum(jnp.where(mine, terms, 0.0), axis=1, keepdims=True)
        out_ref[:, features:] = split_value(value, lane, 0).astype(BF)

    return called(
        body,
        jax.ShapeDtypeStruct((rows, features + 128), BF),
        2 * rows * lines * features,
        grid=(1,),
        in_specs=[
            pl.BlockSpec(memory_space=pltpu.SMEM),
            pl.BlockSpec((lines, features), lambda i: (0, steps)),
            pl.BlockSpec((lines, 128), lambda i: (0, (steps + 1) * features // 128)),
        ],
        out_specs=whole((rows, features + 128)),
    )(masks, third, third)


def pool_gradient(third, asked, pool_hidden, inverse, norm_gain):
    lines, width = third.shape
    pool, features = pool_hidden.shape
    steps = asked.shape[0]
    tile = 256

    def body(third_ref, asked_ref, hidden_ref, inverse_ref, gain_ref, out_ref):
        row = sublanes_of((tile, lines)) + pl.program_id(0) * tile
        delta = jnp.zeros((tile, features), F32)
        value = jnp.zeros((tile, 1), F32)
        lane = lanes_of((tile, 128))
        for t in range(steps):
            back = hot(row == asked_ref[t : t + 1, :])
            delta = delta + dot(back, third_ref[:, t * features : (t + 1) * features])
            terms = dot(back, third_ref[:, width - 128 :])
            mine = (lane >= 3 * t) & (lane < 3 * t + 3)
            value = value + jnp.sum(jnp.where(mine, terms, 0.0), axis=1, keepdims=True)
        gain = gain_ref[...]
        scaled = gain * hidden_ref[...].astype(F32)
        inner = delta - scaled * (inverse_ref[...] * value)
        out_ref[...] = (gain * inverse_ref[...] * inner).astype(BF)

    tiled = lambda n: pl.BlockSpec((tile, n), lambda i: (i, 0))
    return called(
        body,
        jax.ShapeDtypeStruct((pool, features), BF),
        2 * pool * lines * steps * features,
        grid=(pool // tile,),
        in_specs=[
            whole((lines, width)),
            whole((steps, lines)),
            tiled(features),
            tiled(1),
            whole((1, features)),
        ],
        out_specs=tiled(features),
    )(third, asked, pool_hidden, inverse[:, None], norm_gain[None, :])


def per_device(
    query_hidden, positive_hidden, pool_hidden, norm_gain, hard_ids, location, partner_masks
):
    devices = lax.axis_size("batch")
    parts = lax.axis_size("mp")
    me_mp = lax.axis_index("mp")
    rows_dev, feature_dev = query_hidden.shape
    pool_dev = pool_hidden.shape[0]
    hard_count = hard_ids.shape[0] * hard_ids.shape[1]
    capacity = max(hard_count // 32, 2 * ((hard_count + devices - 1) // devices))
    steps = (capacity + GROUP - 1) // GROUP
    chunk = rows_dev // devices
    lines = devices * GROUP
    share = rows_dev // parts
    int_range = lambda n: jnp.arange(n, dtype=jnp.int32)

    partial_squares = row_squares(positive_hidden, norm_gain)
    inverse_p = lax.rsqrt(summed(partial_squares) + EPSILON)
    emb_p = embedding(positive_hidden, norm_gain, inverse_p)

    ids = jnp.where(partial_squares[:, None] < 0.0, 0, hard_ids).T.reshape(-1)
    storage = looked_up(location, ids)
    owners = storage // pool_dev
    local_row = storage % pool_dev
    order = int_range(hard_count)
    earlier = (owners[:, None] == owners[None, :]) & (order[None, :] < order[:, None])
    slot_index = jnp.sum(earlier.astype(jnp.int32), axis=1)
    line = slot_index % GROUP
    group = slot_index // GROUP
    code = group * lines + owners * GROUP + line
    lane = group * (GROUP // chunk) + line // chunk
    lanes = int_range(128)[None, :]
    wanted = local_row + 1
    digits = jnp.where(
        lanes == lane[:, None],
        (wanted >> 4)[:, None],
        jnp.where(lanes == lane[:, None] + 64, (wanted & 15)[:, None], 0),
    ).astype(BF)
    request_line = one_hot(owners * chunk + line % chunk, devices * chunk)
    requests = dot(request_line, digits, ((0,), (0,))).astype(BF)

    packed = jnp.concatenate(
        [emb_p.reshape(devices, chunk, feature_dev), requests.reshape(devices, chunk, 128)], axis=2
    )
    first = exchanged(packed).reshape(rows_dev, feature_dev + 128)
    tie = packed[0, 0, 128:].astype(F32)
    late_gain = jnp.where(jnp.isnan(tie), 0.0, norm_gain)
    squares = lax.psum(
        jnp.concatenate([row_squares(x, late_gain) for x in (query_hidden, pool_hidden)]), "mp"
    )
    inverse_q, inverse_pool = jnp.split(lax.rsqrt(squares + EPSILON), [rows_dev])
    halves = GROUP // chunk
    asked = first[:, feature_dev:].reshape(devices, chunk, 128).astype(jnp.int32)
    asked = asked[:, :, : steps * halves] * 16 + asked[:, :, 64 : 64 + steps * halves] - 1
    asked = asked.reshape(devices, chunk, steps, halves).transpose(2, 0, 3, 1).reshape(steps, lines)

    emb_p = embedding(positive_hidden, norm_gain, after(inverse_p, first))
    emb_q = embedding(query_hidden, norm_gain, inverse_q)
    emb_pool = embedding(pool_hidden, norm_gain, inverse_pool)
    turned_q = lax.dynamic_slice_in_dim(
        jnp.concatenate([emb_q, emb_q], axis=0), me_mp * share, rows_dev
    )

    arrived = exchanged(served_rows(first, emb_pool, partner_masks, steps, chunk))

    own_parts = dot(turned_q, emb_p, ((1,), (1,)))
    scores_own = own_parts[:share]
    for step in range(1, parts):
        scores_own = scores_own + lax.ppermute(
            own_parts[step * share : (step + 1) * share],
            "mp",
            [(i, (i + step) % parts) for i in range(parts)],
        )
    scores_own = scores_own / SOFTMAX_TEMPER
    kept, *coded = partial_scores(turned_q, arrived, code, steps, parts)
    total = jnp.zeros_like(kept)
    for step in range(1, parts):
        total = total + lax.ppermute(
            coded[step - 1], "mp", [(i, (i + step) % parts) for i in range(parts)]
        ).astype(F32)
    scores_far = (kept + total * (1.0 / FIXED)) * (1.0 / SOFTMAX_TEMPER)
    exp_own = jnp.exp(scores_own)
    exp_far = jnp.exp(scores_far)
    sums = jnp.sum(exp_own, axis=1) + jnp.sum(exp_far, axis=1)
    own = int_range(share)[:, None] + me_mp * share == int_range(rows_dev)[None, :]
    losses = jnp.log(sums) - jnp.sum(jnp.where(own, scores_own, 0.0), axis=1)
    ratio = 1.0 / sums
    weights_own = ((exp_own * ratio[:, None] - own.astype(F32)) * SCALE).astype(BF)
    weights_far = (exp_far * ratio[:, None] * SCALE).astype(BF)

    def gathered(piece):
        pieces = [piece]
        for step in range(1, parts):
            pieces.append(
                lax.ppermute(piece, "mp", [((i + step) % parts, i) for i in range(parts)])
            )
        return pieces

    far_pieces = gathered(weights_far)
    values = folded(
        jnp.concatenate(
            [
                jnp.sum(weights_far.astype(F32) * scores_far, axis=0),
                jnp.sum(weights_own.astype(F32) * scores_own, axis=0),
            ]
        )
        * SOFTMAX_TEMPER
    )
    columns = lines + hard_count
    third = exchanged(
        outgoing_rows(far_pieces, code, values[:columns], turned_q, lines, steps)
    )
    weights_own = jnp.concatenate(gathered(weights_own), axis=0)
    weights_far = jnp.concatenate(far_pieces, axis=0)

    def natural(x):
        return lax.dynamic_slice_in_dim(
            jnp.concatenate([x, x], axis=0), (parts - me_mp) * share, rows_dev
        )

    def row_products(hidden, delta):
        return summed(jnp.sum(scaled_rows(hidden, norm_gain) * delta, axis=1))

    weights_slots = dot(weights_far[:, lines:], one_hot(code, steps * lines)).astype(BF)
    weights_slots = jnp.concatenate([weights_slots, weights_far[:, :lines]], axis=1)
    delta_q = dot(weights_own, emb_p)
    for t in range(steps + 1):
        delta_q = delta_q + dot(
            weights_slots[:, t * lines : (t + 1) * lines],
            arrived[:, t * feature_dev : (t + 1) * feature_dev],
        )
    delta_q = natural(delta_q)
    product_q = summed(jnp.sum(scaled_rows(query_hidden, norm_gain) * delta_q, axis=1))
    grad_q = gradient(query_hidden, inverse_q, delta_q, product_q, norm_gain)
    delta_own = dot(weights_own, turned_q, ((0,), (0,)))

    masks = after(after(partner_masks, grad_q), delta_own)
    merged = merged_rows(third, masks, rows_dev, feature_dev, steps, chunk)
    home = exchanged(merged)
    grad_pool = pool_gradient(third, asked, pool_hidden, inverse_pool, norm_gain)
    home = home.astype(F32)
    delta_p = delta_own + home[:, :feature_dev]
    value_p = values[columns:] + jnp.sum(home[:, feature_dev : feature_dev + 3], axis=1)
    grad_p = gradient(positive_hidden, inverse_p, delta_p, value_p / inverse_p, norm_gain)
    return (losses, grad_q, grad_p, grad_pool)


def solution(mesh):
    placed = (
        P("batch", "mp"),
        P("batch", "mp"),
        P("batch", "mp"),
        P("mp"),
        P("batch", None),
        P(),
        P(),
    )
    return jax.shard_map(
        per_device,
        mesh=mesh,
        in_specs=placed,
        out_specs=(P(("batch", "mp")), P("batch", "mp"), P("batch", "mp"), P("batch", "mp")),
        check_vma=False,
    )
```

```python
import jax
import jax.numpy as jnp
from jax import lax
from jax.experimental import pallas as pl
from jax.experimental.pallas import tpu as pltpu
from jax.sharding import PartitionSpec as P

MODEL_WIDTH = 4096
SOFTMAX_TEMPER = 0.02
EPSILON = 1e-06
FIXED = 32000.0
SCALE = MODEL_WIDTH / 64.0 / SOFTMAX_TEMPER
BF = jnp.bfloat16
F32 = jnp.float32


def exchanged(x):
    return lax.all_to_all(x, "batch", split_axis=0, concat_axis=0, tiled=True)


def scaled_rows(hidden, norm_gain):
    return norm_gain[None, :] * hidden.astype(F32)


def row_squares(hidden, norm_gain):
    scaled = scaled_rows(hidden, norm_gain)
    return jnp.sum(scaled * scaled, axis=1)


def embedding(hidden, norm_gain, inverse):
    return (scaled_rows(hidden, norm_gain) * inverse[:, None]).astype(BF)


def gradient(hidden, inverse, delta, product, norm_gain):
    inner = delta - scaled_rows(hidden, norm_gain) * (inverse * inverse * product)[:, None]
    return (norm_gain[None, :] * inverse[:, None] * inner).astype(BF)


def dot(a, b, dims=((1,), (0,))):
    return lax.dot_general(a, b, (dims, ((), ())), preferred_element_type=F32)


def one_hot(column, width):
    return (column[:, None] == jnp.arange(width, dtype=jnp.int32)[None, :]).astype(BF)


def looked_up(table, ids):
    rows = table.shape[0] // 128
    bytes_of = table.reshape(rows, 128)
    parts = jnp.concatenate([bytes_of >> 8, bytes_of & 255], axis=1).astype(BF)
    found = dot(one_hot(ids >> 7, rows), parts)
    value = found[:, :128] * 256.0 + found[:, 128:]
    lane = (ids & 127)[:, None] == jnp.arange(128, dtype=jnp.int32)[None, :]
    return jnp.sum(jnp.where(lane, value, 0.0), axis=1).astype(jnp.int32)


def after(x, value):
    return jnp.where(jnp.isnan(value.reshape(-1)[0].astype(F32)), jnp.zeros_like(x), x)


def folded(x):
    parts = lax.axis_size("mp")
    for bit in range(parts.bit_length() - 1):
        x = x + lax.ppermute(x, "mp", [(i, i ^ 1 << bit) for i in range(parts)])
    return x


def summed(x):
    parts = lax.axis_size("mp")
    total = x
    for step in range(1, parts):
        total = total + lax.ppermute(x, "mp", [(i, (i + step) % parts) for i in range(parts)])
    return total


VMEM_BYTES = 40 * 1024 * 1024
GROUP = 8


def called(body, out_shape, flops, **more):
    return pl.pallas_call(
        body,
        out_shape=out_shape,
        compiler_params=pltpu.CompilerParams(vmem_limit_bytes=VMEM_BYTES),
        cost_estimate=pl.CostEstimate(flops=flops, bytes_accessed=8 << 20, transcendentals=0),
        **more,
    )


def lanes_of(shape):
    return lax.broadcasted_iota(jnp.int32, shape, 1)


def sublanes_of(shape):
    return lax.broadcasted_iota(jnp.int32, shape, 0)


def hot(matches):
    return matches.astype(F32).astype(BF)


def whole(shape):
    return pl.BlockSpec(shape, lambda i: (0,) * len(shape))


def split_value(value, lane, at):
    high = value.astype(BF).astype(F32)
    middle = (value - high).astype(BF).astype(F32)
    low = value - high - middle
    return jnp.where(
        lane == at, high, jnp.where(lane == at + 1, middle, jnp.where(lane == at + 2, low, 0.0))
    )


def served_rows(first, emb_pool, masks, steps, chunk):
    rows, width = first.shape
    pool, features = emb_pool.shape
    lines = rows // chunk * GROUP
    halves = GROUP // chunk
    tile = lines // 2

    def body(masks_ref, first_ref, pool_ref, out_ref):
        line = sublanes_of((tile, 1)) + pl.program_id(0) * tile
        receiver = line // GROUP
        part = (line % GROUP) // chunk
        piece = line % chunk
        home = receiver * chunk + piece
        digits = dot(hot(lanes_of((tile, rows)) == home), first_ref[:, features:])
        lane = lanes_of(digits.shape)
        for step in range(steps):
            place = step * halves + part
            value = jnp.where(lane == place, digits * 16.0, 0.0)
            value = jnp.where(lane == place + 64, digits, value)
            asked = jnp.sum(value, axis=1, keepdims=True).astype(jnp.int32) - 1
            out = dot(hot(lanes_of((tile, pool)) == asked), pool_ref[...]).astype(BF)
            out_ref[:, step * features : (step + 1) * features] = out
        mask = jnp.where(part == 0, masks_ref[0], masks_ref[1])
        chosen = hot(lanes_of((tile, rows)) == (receiver ^ mask) * chunk + piece)
        out_ref[:, steps * features :] = dot(chosen, first_ref[:, :features]).astype(BF)

    width_out = (steps + 1) * features
    return called(
        body,
        pltpu.HBM((lines, width_out), BF),
        2 * lines * steps * pool * features,
        grid=(lines // tile,),
        in_specs=[
            pl.BlockSpec(memory_space=pltpu.SMEM),
            whole((rows, width)),
            whole((pool, features)),
        ],
        out_specs=pl.BlockSpec((tile, width_out), lambda i: (i, 0)),
    )(masks, first, emb_pool)


def partial_scores(turned_q, arrived, code, steps, parts):
    rows, features = turned_q.shape
    lines = arrived.shape[0]
    hard = code.shape[0]
    share = rows // parts

    def body(q_ref, arrived_ref, code_ref, kept_ref, *rest):
        *coded_refs, total_ref = rest
        step = pl.program_id(0)

        def score(candidates, at):
            count = candidates.shape[0]
            partial = dot(q_ref[...], candidates, ((1,), (1,)))
            kept_ref[:, at : at + count] = partial[:share]
            for i, ref in enumerate(coded_refs):
                coded = jnp.round(partial[(i + 1) * share : (i + 2) * share] * FIXED)
                ref[:, at : at + count] = coded.astype(jnp.int32).astype(jnp.int16)

        @pl.when(step == 0)
        def _():
            score(arrived_ref[...], 0)
            total_ref[...] = jnp.zeros_like(total_ref)

        @pl.when(step > 0)
        def _():
            chosen = hot(lanes_of((hard, lines)) + (step - 1) * lines == code_ref[...])
            total_ref[...] += dot(chosen, arrived_ref[...])

        @pl.when(step == steps)
        def _():
            score(total_ref[...].astype(BF), lines)

    columns = lines + hard
    return called(
        body,
        [jax.ShapeDtypeStruct((share, columns), F32)]
        + [jax.ShapeDtypeStruct((share, columns), jnp.int16)] * (parts - 1),
        2 * hard * steps * lines * features,
        grid=(steps + 1,),
        in_specs=[
            whole((rows, features)),
            pl.BlockSpec((lines, features), lambda i: (0, (i + steps) % (steps + 1))),
            whole((hard, 1)),
        ],
        out_specs=[whole((share, columns))] * parts,
        scratch_shapes=[pltpu.VMEM((hard, features), F32)],
    )(turned_q, arrived, code[:, None])


def outgoing_rows(pieces, code, values, turned_q, lines, steps):
    share, columns = pieces[0].shape
    rows, features = turned_q.shape
    hard = code.shape[0]
    tile = lines // 2

    def body(*refs):
        code_ref, near_ref, far_ref, q_ref, out_ref, all_ref = refs[len(pieces) :]
        step = pl.program_id(0)

        @pl.when(step == 0)
        def _():
            for i, ref in enumerate(refs[: len(pieces)]):
                all_ref[i * share : (i + 1) * share, :] = ref[...]

        lane = lanes_of((tile, 128))
        line = sublanes_of((tile, hard)) + step * tile
        extra = jnp.zeros((tile, 128), F32)
        for t in range(steps):
            matches = line + t * lines == code_ref[...]
            value = jnp.sum(jnp.where(matches, far_ref[...], 0.0), axis=1, keepdims=True)
            extra = extra + split_value(value, lane, 3 * t)
            weights = dot(hot(matches), all_ref[:, lines:], ((1,), (1,))).astype(BF)
            out_ref[:, t * features : (t + 1) * features] = dot(weights, q_ref[...]).astype(BF)
        near = sublanes_of((tile, lines)) + step * tile == lanes_of((tile, lines))
        value = jnp.sum(jnp.where(near, near_ref[...], 0.0), axis=1, keepdims=True)
        extra = extra + split_value(value, lane, 3 * steps)
        weights = all_ref[:, pl.ds(pl.multiple_of(step * tile, tile), tile)]
        delta = dot(weights, q_ref[...], ((0,), (0,)))
        out_ref[:, steps * features : (steps + 1) * features] = delta.astype(BF)
        out_ref[:, (steps + 1) * features :] = extra.astype(BF)

    width = (steps + 1) * features + 128
    return called(
        body,
        pltpu.HBM((lines, width), BF),
        2 * lines * (steps + 1) * rows * (hard + features),
        grid=(2,),
        in_specs=[whole((share, columns))] * len(pieces)
        + [whole((1, hard)), whole((1, lines)), whole((1, hard)), whole((rows, features))],
        out_specs=pl.BlockSpec((tile, width), lambda i: (i, 0)),
        scratch_shapes=[pltpu.VMEM((rows, columns), BF)],
    )(
        *pieces,
        code[None, :],
        values[None, :lines],
        values[None, lines:],
        turned_q,
    )


def merged_rows(third, masks, rows, features, steps, chunk):
    lines, width = third.shape

    def body(masks_ref, near_ref, extra_ref, out_ref):
        line = lanes_of((1, lines))
        mask = jnp.where((line % GROUP) // chunk == 0, masks_ref[0], masks_ref[1])
        target = ((line // GROUP) ^ mask) * chunk + line % chunk
        back = hot(sublanes_of((rows, lines)) == target)
        out_ref[:, :features] = dot(back, near_ref[...]).astype(BF)
        lane = lanes_of((rows, 128))
        terms = dot(back, extra_ref[...])
        mine = (lane >= 3 * steps) & (lane < 3 * steps + 3)
        value = jnp.sum(jnp.where(mine, terms, 0.0), axis=1, keepdims=True)
        out_ref[:, features:] = split_value(value, lane, 0).astype(BF)

    return called(
        body,
        jax.ShapeDtypeStruct((rows, features + 128), BF),
        2 * rows * lines * features,
        grid=(1,),
        in_specs=[
            pl.BlockSpec(memory_space=pltpu.SMEM),
            pl.BlockSpec((lines, features), lambda i: (0, steps)),
            pl.BlockSpec((lines, 128), lambda i: (0, (steps + 1) * features // 128)),
        ],
        out_specs=whole((rows, features + 128)),
    )(masks, third, third)


def pool_gradient(third, asked, pool_hidden, inverse, norm_gain):
    lines, width = third.shape
    pool, features = pool_hidden.shape
    steps = asked.shape[0]
    tile = 256

    def body(third_ref, asked_ref, hidden_ref, inverse_ref, gain_ref, out_ref):
        row = sublanes_of((tile, lines)) + pl.program_id(0) * tile
        delta = jnp.zeros((tile, features), F32)
        value = jnp.zeros((tile, 1), F32)
        lane = lanes_of((tile, 128))
        for t in range(steps):
            back = hot(row == asked_ref[t : t + 1, :])
            delta = delta + dot(back, third_ref[:, t * features : (t + 1) * features])
            terms = dot(back, third_ref[:, width - 128 :])
            mine = (lane >= 3 * t) & (lane < 3 * t + 3)
            value = value + jnp.sum(jnp.where(mine, terms, 0.0), axis=1, keepdims=True)
        gain = gain_ref[...]
        scaled = gain * hidden_ref[...].astype(F32)
        inner = delta - scaled * (inverse_ref[...] * value)
        out_ref[...] = (gain * inverse_ref[...] * inner).astype(BF)

    tiled = lambda n: pl.BlockSpec((tile, n), lambda i: (i, 0))
    return called(
        body,
        jax.ShapeDtypeStruct((pool, features), BF),
        2 * pool * lines * steps * features,
        grid=(pool // tile,),
        in_specs=[
            whole((lines, width)),
            whole((steps, lines)),
            tiled(features),
            tiled(1),
            whole((1, features)),
        ],
        out_specs=tiled(features),
    )(third, asked, pool_hidden, inverse[:, None], norm_gain[None, :])


def per_device(
    query_hidden, positive_hidden, pool_hidden, norm_gain, hard_ids, location, partner_masks
):
    devices = lax.axis_size("batch")
    parts = lax.axis_size("mp")
    me_mp = lax.axis_index("mp")
    rows_dev, feature_dev = query_hidden.shape
    pool_dev = pool_hidden.shape[0]
    hard_count = hard_ids.shape[0] * hard_ids.shape[1]
    capacity = max(hard_count // 32, 2 * ((hard_count + devices - 1) // devices))
    steps = (capacity + GROUP - 1) // GROUP
    chunk = rows_dev // devices
    lines = devices * GROUP
    share = rows_dev // parts
    int_range = lambda n: jnp.arange(n, dtype=jnp.int32)

    partial_squares = row_squares(positive_hidden, norm_gain)
    inverse_p = lax.rsqrt(summed(partial_squares) + EPSILON)
    emb_p = embedding(positive_hidden, norm_gain, inverse_p)

    ids = jnp.where(partial_squares[:, None] < 0.0, 0, hard_ids).T.reshape(-1)
    storage = looked_up(location, ids)
    owners = storage // pool_dev
    local_row = storage % pool_dev
    order = int_range(hard_count)
    earlier = (owners[:, None] == owners[None, :]) & (order[None, :] < order[:, None])
    slot_index = jnp.sum(earlier.astype(jnp.int32), axis=1)
    line = slot_index % GROUP
    group = slot_index // GROUP
    code = group * lines + owners * GROUP + line
    lane = group * (GROUP // chunk) + line // chunk
    lanes = int_range(128)[None, :]
    wanted = local_row + 1
    digits = jnp.where(
        lanes == lane[:, None],
        (wanted >> 4)[:, None],
        jnp.where(lanes == lane[:, None] + 64, (wanted & 15)[:, None], 0),
    ).astype(BF)
    request_line = one_hot(owners * chunk + line % chunk, devices * chunk)
    requests = dot(request_line, digits, ((0,), (0,))).astype(BF)

    packed = jnp.concatenate(
        [emb_p.reshape(devices, chunk, feature_dev), requests.reshape(devices, chunk, 128)], axis=2
    )
    first = exchanged(packed).reshape(rows_dev, feature_dev + 128)
    tie = packed[0, 0, 128:].astype(F32)
    late_gain = jnp.where(jnp.isnan(tie), 0.0, norm_gain)
    squares = lax.psum(
        jnp.concatenate([row_squares(x, late_gain) for x in (query_hidden, pool_hidden)]), "mp"
    )
    inverse_q, inverse_pool = jnp.split(lax.rsqrt(squares + EPSILON), [rows_dev])
    halves = GROUP // chunk
    asked = first[:, feature_dev:].reshape(devices, chunk, 128).astype(jnp.int32)
    asked = asked[:, :, : steps * halves] * 16 + asked[:, :, 64 : 64 + steps * halves] - 1
    asked = asked.reshape(devices, chunk, steps, halves).transpose(2, 0, 3, 1).reshape(steps, lines)

    emb_p = embedding(positive_hidden, norm_gain, after(inverse_p, first))
    emb_q = embedding(query_hidden, norm_gain, inverse_q)
    emb_pool = embedding(pool_hidden, norm_gain, inverse_pool)
    turned_q = lax.dynamic_slice_in_dim(
        jnp.concatenate([emb_q, emb_q], axis=0), me_mp * share, rows_dev
    )

    arrived = exchanged(served_rows(first, emb_pool, partner_masks, steps, chunk))

    own_parts = dot(turned_q, emb_p, ((1,), (1,)))
    scores_own = own_parts[:share]
    for step in range(1, parts):
        scores_own = scores_own + lax.ppermute(
            own_parts[step * share : (step + 1) * share],
            "mp",
            [(i, (i + step) % parts) for i in range(parts)],
        )
    scores_own = scores_own / SOFTMAX_TEMPER
    kept, *coded = partial_scores(turned_q, arrived, code, steps, parts)
    total = jnp.zeros_like(kept)
    for step in range(1, parts):
        total = total + lax.ppermute(
            coded[step - 1], "mp", [(i, (i + step) % parts) for i in range(parts)]
        ).astype(F32)
    scores_far = (kept + total * (1.0 / FIXED)) * (1.0 / SOFTMAX_TEMPER)
    exp_own = jnp.exp(scores_own)
    exp_far = jnp.exp(scores_far)
    sums = jnp.sum(exp_own, axis=1) + jnp.sum(exp_far, axis=1)
    own = int_range(share)[:, None] + me_mp * share == int_range(rows_dev)[None, :]
    losses = jnp.log(sums) - jnp.sum(jnp.where(own, scores_own, 0.0), axis=1)
    ratio = 1.0 / sums
    weights_own = ((exp_own * ratio[:, None] - own.astype(F32)) * SCALE).astype(BF)
    weights_far = (exp_far * ratio[:, None] * SCALE).astype(BF)

    def gathered(piece):
        pieces = [piece]
        for step in range(1, parts):
            pieces.append(
                lax.ppermute(piece, "mp", [((i + step) % parts, i) for i in range(parts)])
            )
        return pieces

    far_pieces = gathered(weights_far)
    values = folded(
        jnp.concatenate(
            [
                jnp.sum(weights_far.astype(F32) * scores_far, axis=0),
                jnp.sum(weights_own.astype(F32) * scores_own, axis=0),
            ]
        )
        * SOFTMAX_TEMPER
    )
    columns = lines + hard_count
    third = exchanged(
        outgoing_rows(far_pieces, code, values[:columns], turned_q, lines, steps)
    )
    weights_own = jnp.concatenate(gathered(weights_own), axis=0)
    weights_far = jnp.concatenate(far_pieces, axis=0)

    def natural(x):
        return lax.dynamic_slice_in_dim(
            jnp.concatenate([x, x], axis=0), (parts - me_mp) * share, rows_dev
        )

    def row_products(hidden, delta):
        return summed(jnp.sum(scaled_rows(hidden, norm_gain) * delta, axis=1))

    weights_slots = dot(weights_far[:, lines:], one_hot(code, steps * lines)).astype(BF)
    weights_slots = jnp.concatenate([weights_slots, weights_far[:, :lines]], axis=1)
    delta_q = dot(weights_own, emb_p)
    for t in range(steps + 1):
        delta_q = delta_q + dot(
            weights_slots[:, t * lines : (t + 1) * lines],
            arrived[:, t * feature_dev : (t + 1) * feature_dev],
        )
    delta_q = natural(delta_q)
    product_q = summed(jnp.sum(scaled_rows(query_hidden, norm_gain) * delta_q, axis=1))
    grad_q = gradient(query_hidden, inverse_q, delta_q, product_q, norm_gain)
    delta_own = dot(weights_own, turned_q, ((0,), (0,)))

    masks = after(after(partner_masks, grad_q), delta_own)
    merged = merged_rows(third, masks, rows_dev, feature_dev, steps, chunk)
    home = exchanged(merged)
    grad_pool = pool_gradient(third, asked, pool_hidden, inverse_pool, norm_gain)
    home = home.astype(F32)
    delta_p = delta_own + home[:, :feature_dev]
    value_p = values[columns:] + jnp.sum(home[:, feature_dev : feature_dev + 3], axis=1)
    grad_p = gradient(positive_hidden, inverse_p, delta_p, value_p / inverse_p, norm_gain)
    return (losses, grad_q, grad_p, grad_pool)


def solution(mesh):
    placed = (
        P("batch", "mp"),
        P("batch", "mp"),
        P("batch", "mp"),
        P("mp"),
        P("batch", None),
        P(),
        P(),
    )
    return jax.shard_map(
        per_device,
        mesh=mesh,
        in_specs=placed,
        out_specs=(P(("batch", "mp")), P("batch", "mp"), P("batch", "mp"), P("batch", "mp")),
        check_vma=False,
    )
```

```python
import jax
import jax.numpy as jnp
from jax import lax
from jax.experimental import pallas as pl
from jax.experimental.pallas import tpu as pltpu
from jax.sharding import PartitionSpec as P

MODEL_WIDTH = 4096
SOFTMAX_TEMPER = 0.02
EPSILON = 1e-06
FIXED = 32000.0
SCALE = MODEL_WIDTH / 64.0 / SOFTMAX_TEMPER
BF = jnp.bfloat16
F32 = jnp.float32


def exchanged(x):
    return lax.all_to_all(x, "batch", split_axis=0, concat_axis=0, tiled=True)


def scaled_rows(hidden, norm_gain):
    return norm_gain[None, :] * hidden.astype(F32)


def row_squares(hidden, norm_gain):
    scaled = scaled_rows(hidden, norm_gain)
    return jnp.sum(scaled * scaled, axis=1)


def embedding(hidden, norm_gain, inverse):
    return (scaled_rows(hidden, norm_gain) * inverse[:, None]).astype(BF)


def gradient(hidden, inverse, delta, product, norm_gain):
    inner = delta - scaled_rows(hidden, norm_gain) * (inverse * inverse * product)[:, None]
    return (norm_gain[None, :] * inverse[:, None] * inner).astype(BF)


def dot(a, b, dims=((1,), (0,))):
    return lax.dot_general(a, b, (dims, ((), ())), preferred_element_type=F32)


def one_hot(column, width):
    return (column[:, None] == jnp.arange(width, dtype=jnp.int32)[None, :]).astype(BF)


def looked_up(table, ids):
    rows = table.shape[0] // 128
    bytes_of = table.reshape(rows, 128)
    parts = jnp.concatenate([bytes_of >> 8, bytes_of & 255], axis=1).astype(BF)
    found = dot(one_hot(ids >> 7, rows), parts)
    value = found[:, :128] * 256.0 + found[:, 128:]
    lane = (ids & 127)[:, None] == jnp.arange(128, dtype=jnp.int32)[None, :]
    return jnp.sum(jnp.where(lane, value, 0.0), axis=1).astype(jnp.int32)


def after(x, value):
    return jnp.where(jnp.isnan(value.reshape(-1)[0].astype(F32)), jnp.zeros_like(x), x)


def folded(x):
    parts = lax.axis_size("mp")
    for bit in range(parts.bit_length() - 1):
        x = x + lax.ppermute(x, "mp", [(i, i ^ 1 << bit) for i in range(parts)])
    return x


def summed(x):
    parts = lax.axis_size("mp")
    total = x
    for step in range(1, parts):
        total = total + lax.ppermute(x, "mp", [(i, (i + step) % parts) for i in range(parts)])
    return total


VMEM_BYTES = 40 * 1024 * 1024
GROUP = 8


def called(body, out_shape, flops, **more):
    return pl.pallas_call(
        body,
        out_shape=out_shape,
        compiler_params=pltpu.CompilerParams(vmem_limit_bytes=VMEM_BYTES),
        cost_estimate=pl.CostEstimate(flops=flops, bytes_accessed=8 << 20, transcendentals=0),
        **more,
    )


def lanes_of(shape):
    return lax.broadcasted_iota(jnp.int32, shape, 1)


def sublanes_of(shape):
    return lax.broadcasted_iota(jnp.int32, shape, 0)


def hot(matches):
    return matches.astype(F32).astype(BF)


def whole(shape):
    return pl.BlockSpec(shape, lambda i: (0,) * len(shape))


def split_value(value, lane, at):
    high = value.astype(BF).astype(F32)
    middle = (value - high).astype(BF).astype(F32)
    low = value - high - middle
    return jnp.where(
        lane == at, high, jnp.where(lane == at + 1, middle, jnp.where(lane == at + 2, low, 0.0))
    )


def served_rows(first, emb_pool, masks, steps, chunk):
    rows, width = first.shape
    pool, features = emb_pool.shape
    lines = rows // chunk * GROUP
    halves = GROUP // chunk
    tile = lines // 2

    def body(masks_ref, first_ref, pool_ref, out_ref):
        line = sublanes_of((tile, 1)) + pl.program_id(0) * tile
        receiver = line // GROUP
        part = (line % GROUP) // chunk
        piece = line % chunk
        home = receiver * chunk + piece
        digits = dot(hot(lanes_of((tile, rows)) == home), first_ref[:, features:])
        lane = lanes_of(digits.shape)
        for step in range(steps):
            place = step * halves + part
            value = jnp.where(lane == place, digits * 16.0, 0.0)
            value = jnp.where(lane == place + 64, digits, value)
            asked = jnp.sum(value, axis=1, keepdims=True).astype(jnp.int32) - 1
            out = dot(hot(lanes_of((tile, pool)) == asked), pool_ref[...]).astype(BF)
            out_ref[:, step * features : (step + 1) * features] = out
        mask = jnp.where(part == 0, masks_ref[0], masks_ref[1])
        chosen = hot(lanes_of((tile, rows)) == (receiver ^ mask) * chunk + piece)
        out_ref[:, steps * features :] = dot(chosen, first_ref[:, :features]).astype(BF)

    width_out = (steps + 1) * features
    return called(
        body,
        pltpu.HBM((lines, width_out), BF),
        2 * lines * steps * pool * features,
        grid=(lines // tile,),
        in_specs=[
            pl.BlockSpec(memory_space=pltpu.SMEM),
            whole((rows, width)),
            whole((pool, features)),
        ],
        out_specs=pl.BlockSpec((tile, width_out), lambda i: (i, 0)),
    )(masks, first, emb_pool)


def partial_scores(turned_q, arrived, code, steps, parts):
    rows, features = turned_q.shape
    lines = arrived.shape[0]
    hard = code.shape[0]
    share = rows // parts

    def body(q_ref, arrived_ref, code_ref, kept_ref, *rest):
        *coded_refs, total_ref = rest
        step = pl.program_id(0)

        def score(candidates, at):
            count = candidates.shape[0]
            partial = dot(q_ref[...], candidates, ((1,), (1,)))
            kept_ref[:, at : at + count] = partial[:share]
            for i, ref in enumerate(coded_refs):
                coded = jnp.round(partial[(i + 1) * share : (i + 2) * share] * FIXED)
                ref[:, at : at + count] = coded.astype(jnp.int32).astype(jnp.int16)

        @pl.when(step == 0)
        def _():
            score(arrived_ref[...], 0)
            total_ref[...] = jnp.zeros_like(total_ref)

        @pl.when(step > 0)
        def _():
            chosen = hot(lanes_of((hard, lines)) + (step - 1) * lines == code_ref[...])
            total_ref[...] += dot(chosen, arrived_ref[...])

        @pl.when(step == steps)
        def _():
            score(total_ref[...].astype(BF), lines)

    columns = lines + hard
    return called(
        body,
        [jax.ShapeDtypeStruct((share, columns), F32)]
        + [jax.ShapeDtypeStruct((share, columns), jnp.int16)] * (parts - 1),
        2 * hard * steps * lines * features,
        grid=(steps + 1,),
        in_specs=[
            whole((rows, features)),
            pl.BlockSpec((lines, features), lambda i: (0, (i + steps) % (steps + 1))),
            whole((hard, 1)),
        ],
        out_specs=[whole((share, columns))] * parts,
        scratch_shapes=[pltpu.VMEM((hard, features), F32)],
    )(turned_q, arrived, code[:, None])


def outgoing_rows(pieces, code, values, turned_q, lines, steps):
    share, columns = pieces[0].shape
    rows, features = turned_q.shape
    hard = code.shape[0]
    tile = lines // 2

    def body(*refs):
        code_ref, near_ref, far_ref, q_ref, out_ref, all_ref = refs[len(pieces) :]
        step = pl.program_id(0)

        @pl.when(step == 0)
        def _():
            for i, ref in enumerate(refs[: len(pieces)]):
                all_ref[i * share : (i + 1) * share, :] = ref[...]

        lane = lanes_of((tile, 128))
        line = sublanes_of((tile, hard)) + step * tile
        extra = jnp.zeros((tile, 128), F32)
        for t in range(steps):
            matches = line + t * lines == code_ref[...]
            value = jnp.sum(jnp.where(matches, far_ref[...], 0.0), axis=1, keepdims=True)
            extra = extra + split_value(value, lane, 3 * t)
            weights = dot(hot(matches), all_ref[:, lines:], ((1,), (1,))).astype(BF)
            out_ref[:, t * features : (t + 1) * features] = dot(weights, q_ref[...]).astype(BF)
        near = sublanes_of((tile, lines)) + step * tile == lanes_of((tile, lines))
        value = jnp.sum(jnp.where(near, near_ref[...], 0.0), axis=1, keepdims=True)
        extra = extra + split_value(value, lane, 3 * steps)
        weights = all_ref[:, pl.ds(pl.multiple_of(step * tile, tile), tile)]
        delta = dot(weights, q_ref[...], ((0,), (0,)))
        out_ref[:, steps * features : (steps + 1) * features] = delta.astype(BF)
        out_ref[:, (steps + 1) * features :] = extra.astype(BF)

    width = (steps + 1) * features + 128
    return called(
        body,
        pltpu.HBM((lines, width), BF),
        2 * lines * (steps + 1) * rows * (hard + features),
        grid=(2,),
        in_specs=[whole((share, columns))] * len(pieces)
        + [whole((1, hard)), whole((1, lines)), whole((1, hard)), whole((rows, features))],
        out_specs=pl.BlockSpec((tile, width), lambda i: (i, 0)),
        scratch_shapes=[pltpu.VMEM((rows, columns), BF)],
    )(
        *pieces,
        code[None, :],
        values[None, :lines],
        values[None, lines:],
        turned_q,
    )


def merged_rows(third, masks, rows, features, steps, chunk):
    lines, width = third.shape

    def body(masks_ref, near_ref, extra_ref, out_ref):
        line = lanes_of((1, lines))
        mask = jnp.where((line % GROUP) // chunk == 0, masks_ref[0], masks_ref[1])
        target = ((line // GROUP) ^ mask) * chunk + line % chunk
        back = hot(sublanes_of((rows, lines)) == target)
        out_ref[:, :features] = dot(back, near_ref[...]).astype(BF)
        lane = lanes_of((rows, 128))
        terms = dot(back, extra_ref[...])
        mine = (lane >= 3 * steps) & (lane < 3 * steps + 3)
        value = jnp.sum(jnp.where(mine, terms, 0.0), axis=1, keepdims=True)
        out_ref[:, features:] = split_value(value, lane, 0).astype(BF)

    return called(
        body,
        jax.ShapeDtypeStruct((rows, features + 128), BF),
        2 * rows * lines * features,
        grid=(1,),
        in_specs=[
            pl.BlockSpec(memory_space=pltpu.SMEM),
            pl.BlockSpec((lines, features), lambda i: (0, steps)),
            pl.BlockSpec((lines, 128), lambda i: (0, (steps + 1) * features // 128)),
        ],
        out_specs=whole((rows, features + 128)),
    )(masks, third, third)


def pool_gradient(third, asked, pool_hidden, inverse, norm_gain):
    lines, width = third.shape
    pool, features = pool_hidden.shape
    steps = asked.shape[0]
    tile = 256

    def body(third_ref, asked_ref, hidden_ref, inverse_ref, gain_ref, out_ref):
        row = sublanes_of((tile, lines)) + pl.program_id(0) * tile
        delta = jnp.zeros((tile, features), F32)
        value = jnp.zeros((tile, 1), F32)
        lane = lanes_of((tile, 128))
        for t in range(steps):
            back = hot(row == asked_ref[t : t + 1, :])
            delta = delta + dot(back, third_ref[:, t * features : (t + 1) * features])
            terms = dot(back, third_ref[:, width - 128 :])
            mine = (lane >= 3 * t) & (lane < 3 * t + 3)
            value = value + jnp.sum(jnp.where(mine, terms, 0.0), axis=1, keepdims=True)
        gain = gain_ref[...]
        scaled = gain * hidden_ref[...].astype(F32)
        inner = delta - scaled * (inverse_ref[...] * value)
        out_ref[...] = (gain * inverse_ref[...] * inner).astype(BF)

    tiled = lambda n: pl.BlockSpec((tile, n), lambda i: (i, 0))
    return called(
        body,
        jax.ShapeDtypeStruct((pool, features), BF),
        2 * pool * lines * steps * features,
        grid=(pool // tile,),
        in_specs=[
            whole((lines, width)),
            whole((steps, lines)),
            tiled(features),
            tiled(1),
            whole((1, features)),
        ],
        out_specs=tiled(features),
    )(third, asked, pool_hidden, inverse[:, None], norm_gain[None, :])


def per_device(
    query_hidden, positive_hidden, pool_hidden, norm_gain, hard_ids, location, partner_masks
):
    devices = lax.axis_size("batch")
    parts = lax.axis_size("mp")
    me_mp = lax.axis_index("mp")
    rows_dev, feature_dev = query_hidden.shape
    pool_dev = pool_hidden.shape[0]
    hard_count = hard_ids.shape[0] * hard_ids.shape[1]
    capacity = max(hard_count // 32, 2 * ((hard_count + devices - 1) // devices))
    steps = (capacity + GROUP - 1) // GROUP
    chunk = rows_dev // devices
    lines = devices * GROUP
    share = rows_dev // parts
    int_range = lambda n: jnp.arange(n, dtype=jnp.int32)

    partial_squares = row_squares(positive_hidden, norm_gain)
    inverse_p = lax.rsqrt(summed(partial_squares) + EPSILON)
    emb_p = embedding(positive_hidden, norm_gain, inverse_p)

    ids = jnp.where(partial_squares[:, None] < 0.0, 0, hard_ids).T.reshape(-1)
    storage = looked_up(location, ids)
    owners = storage // pool_dev
    local_row = storage % pool_dev
    order = int_range(hard_count)
    earlier = (owners[:, None] == owners[None, :]) & (order[None, :] < order[:, None])
    slot_index = jnp.sum(earlier.astype(jnp.int32), axis=1)
    line = slot_index % GROUP
    group = slot_index // GROUP
    code = group * lines + owners * GROUP + line
    lane = group * (GROUP // chunk) + line // chunk
    lanes = int_range(128)[None, :]
    wanted = local_row + 1
    digits = jnp.where(
        lanes == lane[:, None],
        (wanted >> 4)[:, None],
        jnp.where(lanes == lane[:, None] + 64, (wanted & 15)[:, None], 0),
    ).astype(BF)
    request_line = one_hot(owners * chunk + line % chunk, devices * chunk)
    requests = dot(request_line, digits, ((0,), (0,))).astype(BF)

    packed = jnp.concatenate(
        [emb_p.reshape(devices, chunk, feature_dev), requests.reshape(devices, chunk, 128)], axis=2
    )
    first = exchanged(packed).reshape(rows_dev, feature_dev + 128)
    tie = packed[0, 0, 128:].astype(F32)
    late_gain = jnp.where(jnp.isnan(tie), 0.0, norm_gain)
    squares = lax.psum(
        jnp.concatenate([row_squares(x, late_gain) for x in (query_hidden, pool_hidden)]), "mp"
    )
    inverse_q, inverse_pool = jnp.split(lax.rsqrt(squares + EPSILON), [rows_dev])
    halves = GROUP // chunk
    asked = first[:, feature_dev:].reshape(devices, chunk, 128).astype(jnp.int32)
    asked = asked[:, :, : steps * halves] * 16 + asked[:, :, 64 : 64 + steps * halves] - 1
    asked = asked.reshape(devices, chunk, steps, halves).transpose(2, 0, 3, 1).reshape(steps, lines)

    emb_p = embedding(positive_hidden, norm_gain, after(inverse_p, first))
    emb_q = embedding(query_hidden, norm_gain, inverse_q)
    emb_pool = embedding(pool_hidden, norm_gain, inverse_pool)
    turned_q = lax.dynamic_slice_in_dim(
        jnp.concatenate([emb_q, emb_q], axis=0), me_mp * share, rows_dev
    )

    arrived = exchanged(served_rows(first, emb_pool, partner_masks, steps, chunk))

    own_parts = dot(turned_q, emb_p, ((1,), (1,)))
    scores_own = own_parts[:share]
    for step in range(1, parts):
        scores_own = scores_own + lax.ppermute(
            own_parts[step * share : (step + 1) * share],
            "mp",
            [(i, (i + step) % parts) for i in range(parts)],
        )
    scores_own = scores_own / SOFTMAX_TEMPER
    kept, *coded = partial_scores(turned_q, arrived, code, steps, parts)
    total = jnp.zeros_like(kept)
    by_distance = sorted(range(1, parts), key=lambda step: min(step, parts - step))
    for step in by_distance:
        total = total + lax.ppermute(
            coded[step - 1], "mp", [(i, (i + step) % parts) for i in range(parts)]
        ).astype(F32)
    scores_far = (kept + total * (1.0 / FIXED)) * (1.0 / SOFTMAX_TEMPER)
    exp_own = jnp.exp(scores_own)
    exp_far = jnp.exp(scores_far)
    sums = jnp.sum(exp_own, axis=1) + jnp.sum(exp_far, axis=1)
    own = int_range(share)[:, None] + me_mp * share == int_range(rows_dev)[None, :]
    losses = jnp.log(sums) - jnp.sum(jnp.where(own, scores_own, 0.0), axis=1)
    ratio = 1.0 / sums
    weights_own = ((exp_own * ratio[:, None] - own.astype(F32)) * SCALE).astype(BF)
    weights_far = (exp_far * ratio[:, None] * SCALE).astype(BF)

    def gathered(piece):
        pieces = {0: piece}
        for step in by_distance:
            pieces[step] = lax.ppermute(
                piece, "mp", [((i + step) % parts, i) for i in range(parts)]
            )
        return [pieces[step] for step in range(parts)]

    far_pieces = gathered(weights_far)
    values = folded(
        jnp.concatenate(
            [
                jnp.sum(weights_far.astype(F32) * scores_far, axis=0),
                jnp.sum(weights_own.astype(F32) * scores_own, axis=0),
            ]
        )
        * SOFTMAX_TEMPER
    )
    columns = lines + hard_count
    third = exchanged(
        outgoing_rows(far_pieces, code, values[:columns], turned_q, lines, steps)
    )
    weights_own = jnp.concatenate(gathered(weights_own), axis=0)
    weights_far = jnp.concatenate(far_pieces, axis=0)

    def natural(x):
        return lax.dynamic_slice_in_dim(
            jnp.concatenate([x, x], axis=0), (parts - me_mp) * share, rows_dev
        )

    def row_products(hidden, delta):
        return summed(jnp.sum(scaled_rows(hidden, norm_gain) * delta, axis=1))

    weights_slots = dot(weights_far[:, lines:], one_hot(code, steps * lines)).astype(BF)
    weights_slots = jnp.concatenate([weights_slots, weights_far[:, :lines]], axis=1)
    delta_q = dot(weights_own, emb_p)
    for t in range(steps + 1):
        delta_q = delta_q + dot(
            weights_slots[:, t * lines : (t + 1) * lines],
            arrived[:, t * feature_dev : (t + 1) * feature_dev],
        )
    delta_q = natural(delta_q)
    product_q = summed(jnp.sum(scaled_rows(query_hidden, norm_gain) * delta_q, axis=1))
    grad_q = gradient(query_hidden, inverse_q, delta_q, product_q, norm_gain)
    delta_own = dot(weights_own, turned_q, ((0,), (0,)))

    masks = after(after(partner_masks, grad_q), delta_own)
    merged = merged_rows(third, masks, rows_dev, feature_dev, steps, chunk)
    home = exchanged(merged)
    grad_pool = pool_gradient(third, asked, pool_hidden, inverse_pool, norm_gain)
    home = home.astype(F32)
    delta_p = delta_own + home[:, :feature_dev]
    value_p = values[columns:] + jnp.sum(home[:, feature_dev : feature_dev + 3], axis=1)
    grad_p = gradient(positive_hidden, inverse_p, delta_p, value_p / inverse_p, norm_gain)
    return (losses, grad_q, grad_p, grad_pool)


def solution(mesh):
    placed = (
        P("batch", "mp"),
        P("batch", "mp"),
        P("batch", "mp"),
        P("mp"),
        P("batch", None),
        P(),
        P(),
    )
    return jax.shard_map(
        per_device,
        mesh=mesh,
        in_specs=placed,
        out_specs=(P(("batch", "mp")), P("batch", "mp"), P("batch", "mp"), P("batch", "mp")),
        check_vma=False,
    )
```
